32 devices in a mesh: wide: 8 (over y, x, core), narrow: 4 (over z).
Axes of the slice: x: 2, y: 2, z: 4, core: 2. Of those that a mesh axis runs over, the one named last changes fastest.
Arguments:
- coefficients: float32 [7, 7, 7, 32768], P(None, None, None, ('wide', 'narrow')), may hold values from -0.9 to 0.9
- degree: int32 [32768], P(('wide', 'narrow')), may hold values from 2 to 6
- new_degree: int32 [32768], P(('wide', 'narrow')), may hold values from 2 to 6
- face_link: int32 [6, 32768], P(None, ('wide', 'narrow')), may hold values from -1 to 1151, as said below
- send_index: int32 [4, 4096], P(None, ('wide', 'narrow')), may hold values from 0 to 1023, as said below
- new_owner: int32 [32768, 1], P(('wide', 'narrow')), may hold values from 0 to 31; in each aligned block of 1024 rows (0 to 1023, 1024 to 2047, ...) at most 64 rows name the same one
Outputs:
- moved: float32 [7, 7, 7, 65536], P(None, None, None, ('wide', 'narrow'))
The draws below stay inside these ranges and needn't reach their ends.
Inputs may be any that keep to these rules, and one draw needn't show every extreme that they name: `face_link`: faces are numbered 0, 1 (lower, upper x), 2, 3 (y), 4, 5 (z). Each device holds a box of 8 x 16 x 8 elements of a grid; the box across its x sides belongs to the device with the previous or next index of wide and the same narrow index, across its z sides to the device with the previous or next index of narrow and the same wide index. A value below 1024 names the neighbour among the same device's elements; a value 1024 + t names slot t of the neighbouring device's row of send_index (row 1, 0, 3, 2 for faces 0, 1, 4, 5); -1 marks the grid's outer boundary. The neighbour across face f sees the element across its face f xor 1. `send_index`: row 0, 1, 2, 3 lists the device's elements on the lower x, upper x, lower z, upper z side of its box, each once, in the slot order that face_link uses. `new_owner`: the elements of one device name any one device (itself included) at most 64 times, and some device is named exactly 64 times.
All inputs are finite; a program needn't handle non-finite values.
Results may differ from the reference program's by a relative error of at most 0.0003.
Values sent between devices are 32-bit elements; how exact they have to be, the bound alone decides.
A program may use at most 192 MiB of HBM per device.

```python
import math
import jax
import jax.numpy as jnp
import numpy as np
from jax import lax

MODES = 7
QUAD = 8
SIDE = 8
DEPTH = 16
ELEM_DEV = 1024
SLOTS = 128
CAPR = 64
ELEMS = 32768
N_WIDE = 8
N_NARROW = 4


def box_layout(key):
    devices = N_WIDE * N_NARROW
    flips = jax.random.randint(key, (devices,), 0, ELEM_DEV).astype(jnp.int32)
    return flips


def local_index(x_cell, y_cell, z_cell, flip_all):
    return jnp.bitwise_xor(x_cell * DEPTH * SIDE + y_cell * SIDE + z_cell, flip_all)


def draw_face_link(key, part):
    flips = box_layout(key)
    total = N_WIDE * N_NARROW * ELEM_DEV
    ranks = jnp.arange(total, dtype=jnp.int32) // ELEM_DEV
    local = jnp.arange(total, dtype=jnp.int32) % ELEM_DEV
    flip_all = flips[ranks]
    cell = jnp.bitwise_xor(local, flip_all)
    x_cell = cell // (DEPTH * SIDE)
    y_cell = cell // SIDE % DEPTH
    z_cell = cell % SIDE
    wide_pos = ranks // N_NARROW
    narrow_pos = ranks % N_NARROW
    x_slot = ELEM_DEV + y_cell * SIDE + z_cell
    z_slot = ELEM_DEV + x_cell * DEPTH + y_cell
    lower_x = jnp.where(x_cell > 0, local_index(x_cell - 1, y_cell, z_cell, flip_all), jnp.where(wide_pos > 0, x_slot, -1))
    upper_x = jnp.where(x_cell < SIDE - 1, local_index(x_cell + 1, y_cell, z_cell, flip_all), jnp.where(wide_pos < N_WIDE - 1, x_slot, -1))
    lower_y = jnp.where(y_cell > 0, local_index(x_cell, y_cell - 1, z_cell, flip_all), -1)
    upper_y = jnp.where(y_cell < DEPTH - 1, local_index(x_cell, y_cell + 1, z_cell, flip_all), -1)
    lower_z = jnp.where(z_cell > 0, local_index(x_cell, y_cell, z_cell - 1, flip_all), jnp.where(narrow_pos > 0, z_slot, -1))
    upper_z = jnp.where(z_cell < SIDE - 1, local_index(x_cell, y_cell, z_cell + 1, flip_all), jnp.where(narrow_pos < N_NARROW - 1, z_slot, -1))
    return jnp.stack([lower_x, upper_x, lower_y, upper_y, lower_z, upper_z]).astype(jnp.int32)


def draw_send_index(key, part):
    flips = box_layout(key)
    total = N_WIDE * N_NARROW * SLOTS
    ranks = jnp.arange(total, dtype=jnp.int32) // SLOTS
    slot = jnp.arange(total, dtype=jnp.int32) % SLOTS
    flip_all = flips[ranks]
    plane_y = slot // SIDE
    plane_z = slot % SIDE
    depth_x = slot // DEPTH
    depth_y = slot % DEPTH
    lower_x = local_index(jnp.zeros_like(slot), plane_y, plane_z, flip_all)
    upper_x = local_index(jnp.zeros_like(slot) + SIDE - 1, plane_y, plane_z, flip_all)
    lower_z = local_index(depth_x, depth_y, jnp.zeros_like(slot), flip_all)
    upper_z = local_index(depth_x, depth_y, jnp.zeros_like(slot) + SIDE - 1, flip_all)
    return jnp.stack([lower_x, upper_x, lower_z, upper_z]).astype(jnp.int32)


def set_ends(array, rng, low, high):
    longest = array.shape.index(max(array.shape))
    spots = []
    for shift in (0, 1):
        where = [jax.random.randint(jax.random.fold_in(rng, axis), (), 0, length) for axis, length in enumerate(array.shape)]
        where[longest] = (where[longest] + shift) % array.shape[longest]
        spots.append(tuple(where))
    return array.at[spots[0]].set(low).at[spots[1]].set(high)


def block_scale(stream_key, dims, shards, low, top_value):
    def one(axis_at, parts):
        draws = jax.random.uniform(jax.random.fold_in(jax.random.fold_in(stream_key, 6), axis_at), (parts,), jnp.float32, low / len(shards), top_value / len(shards))
        return jnp.repeat(jnp.exp(draws), dims[axis_at] // parts).reshape((-1,) + (1,) * (len(dims) - axis_at - 1))

    loudness = one(*shards[0])
    for cut in shards[1:]:
        loudness = loudness * one(*cut)
    return loudness


def routed_block(key, own, number, rows, count, top, most, lean):
    order = jax.random.permutation(key, count)
    packed, common = shares(count, rows * top, most, lean, True), shares(count, rows * top, most, lean, False)
    places = jnp.arange(count)

    def named(sizes, rotation):
        used = int((sizes > 0).sum())
        fixed = max(1, used // 4)
        passed = fixed + (places - fixed + rotation * (used - fixed)) % max(1, count - fixed)
        return jnp.zeros((count,), jnp.int32).at[order[jnp.where(places < fixed, places, passed)]].set(jnp.asarray(sizes, jnp.int32))

    sizes = jnp.where(number % 4 == 0, named(packed, number // 4), named(common, number - number // 4 - 1))
    mixed = jax.random.permutation(jax.random.fold_in(own, 3), count)
    source_of, sink = mixed[0:count // 2 * 2:2], mixed[1:count // 2 * 2:2]
    room = jnp.minimum(sizes[source_of] - 1, most - sizes[sink]) // 2
    room = jnp.where((source_of == order[0]) | (sink == order[0]) | (sizes[sink] == 0), 0, jnp.maximum(room, 0))
    passed = jax.random.randint(jax.random.fold_in(own, 4), (count // 2,), 0, 1 << 20) % (room + 1)
    sizes = sizes.at[source_of].add(-passed).at[sink].add(passed)
    labels = jnp.searchsorted(jnp.cumsum(sizes), jnp.arange(rows * top), side="right").astype(jnp.int32)
    listing = labels.reshape(top, rows).T
    listing = listing[jax.random.permutation(jax.random.fold_in(own, 1), rows)]
    rotation = jax.random.randint(jax.random.fold_in(own, 2), (rows, 1), 0, top)
    return jnp.take_along_axis(listing, (jnp.arange(top)[None, :] + rotation) % top, axis=1)


def shares(count, total, limit, lean, full):
    loads = [(1 << 20) // math.isqrt(standing ** lean) + 1 for standing in range(1, count + 1)]
    largest = limit if full else min(limit, max(-(-total // count), total * loads[0] // sum(loads)))
    least = 1 if total - largest >= count - 1 else 0
    counts, spare = [largest] + [least] * (count - 1), total - largest - least * (count - 1)
    while spare > 0:
        free = [i for i in range(1, count) if counts[i] < largest] or [i for i in range(1, count) if counts[i] < limit]
        mass, budget = sum([loads[i] for i in free]), spare
        for i in free:
            more = min(limit - counts[i], max(1, budget * loads[i] // mass), spare)
            counts[i] = counts[i] + more
            spare = spare - more
    return np.array(counts)


def centred(own_key, dims, deviation, reach, cuts=(), kind=jnp.bfloat16):
    gain = block_scale(own_key, dims, cuts, -0.22, 0.18) if cuts else 1.0
    entries = jax.random.normal(own_key, dims, jnp.float32) * deviation * gain
    return jnp.minimum(jnp.maximum(entries, -reach), reach).astype(kind)


def setup_inputs(seed: int = 0) -> dict:
    key_list = jax.random.split(jax.random.key(seed), 7)
    coefficients = centred(key_list[0], (MODES, MODES, MODES, ELEMS), 0.15, 0.9, ((3, 32),), jnp.float32)
    degree = set_ends(jax.random.randint(key_list[1], (ELEMS,), 2, 7), jax.random.fold_in(key_list[1], 1), 2, 6).astype(jnp.int32)
    new_degree = set_ends(jax.random.randint(key_list[2], (ELEMS,), 2, 7), jax.random.fold_in(key_list[2], 1), 2, 6).astype(jnp.int32)
    face_link = draw_face_link(jax.random.fold_in(key_list[6], 71), 0)
    send_index = draw_send_index(jax.random.fold_in(key_list[6], 71), 0)
    new_owner_keys = jax.random.split(jax.random.fold_in(key_list[5], 1), ELEMS // ELEM_DEV)
    new_owner_turns = jax.random.permutation(jax.random.fold_in(key_list[5], 3), ELEMS // ELEM_DEV)
    new_owner = jax.vmap(lambda own, number: routed_block(jax.random.fold_in(key_list[5], 2), own, number, ELEM_DEV, N_WIDE * N_NARROW, 1, CAPR, 2))(new_owner_keys, new_owner_turns).reshape((ELEMS, 1))
    return dict(coefficients=coefficients, degree=degree, new_degree=new_degree, face_link=face_link, send_index=send_index, new_owner=new_owner)


HIGH = lax.Precision.HIGHEST
STEP_SIZE = 0.0003
FORMS = ('ti,ijke->tjke', 'tj,ijke->tike', 'tk,ijke->tije')
ADDS = ('ti,tjke->ijke', 'tj,tike->ijke', 'tk,tije->ijke')

def legendre_rows(points, count):
    values = [points * 0.0 + 1.0, points.copy()]
    slopes = [points * 0.0, points * 0.0 + 1.0]
    for order in range(1, count):
        values.append(((2.0 * order + 1.0) * points * values[order] - order * values[order - 1]) / (order + 1.0))
        slopes.append(slopes[order - 1] + (2.0 * order + 1.0) * values[order])
    return (np.stack(values[:count + 1]), np.stack(slopes[:count + 1]))

def gauss_rule(count):
    points = np.cos(np.pi * (np.arange(count) + 0.75) / (count + 0.5))
    for sweep in range(60):
        values, slopes = legendre_rows(points, count)
        points = points - values[count] / slopes[count]
    values, slopes = legendre_rows(points, count)
    weights = 2.0 / ((1.0 - points * points) * slopes[count] ** 2)
    return (points[::-1], weights[::-1])

def basis_tables(modes, quad):
    points, weights = gauss_rule(quad)
    scales = np.sqrt((2.0 * np.arange(modes) + 1.0) / 2.0)
    value_rows, slope_rows = legendre_rows(points, modes)
    values = value_rows[:modes].T * scales
    slopes = slope_rows[:modes].T * scales
    stiffness = slopes.T @ (weights[:, None] * slopes)
    project = (values * weights[:, None]).T
    orders = np.arange(modes)
    edge_values = np.stack([(-1.0) ** orders, np.ones(modes)]) * scales
    edge_slopes = np.stack([(-1.0) ** (orders + 1), np.ones(modes)]) * (orders * (orders + 1) / 2.0) * scales
    return (jnp.asarray(values, jnp.float32), jnp.asarray(project, jnp.float32), jnp.asarray(stiffness, jnp.float32), jnp.asarray(edge_values, jnp.float32), jnp.asarray(edge_slopes, jnp.float32))

def degree_mask(degree, modes):
    order = jnp.arange(modes, dtype=jnp.int32)
    highest = jnp.maximum(jnp.maximum(order[:, None, None], order[None, :, None]), order[None, None, :])
    return (highest[..., None] <= degree[None, None, None, :]).astype(jnp.float32)

def along_all(matrix, field):
    field = jnp.einsum('qi,ijke->qjke', matrix, field, precision=HIGH)
    field = jnp.einsum('rj,qjke->qrke', matrix, field, precision=HIGH)
    return jnp.einsum('sk,qrke->qrse', matrix, field, precision=HIGH)

def kirchhoff(field, mask, tables):
    point_values = along_all(tables[0], field)
    transformed = point_values + point_values ** 3 / 3.0
    return mask * along_all(tables[1], transformed)

def face_traces(field, tables):
    result = []
    for axis in range(3):
        for side in range(2):
            vectors = jnp.stack([tables[3][side], tables[4][side]])
            result.append(jnp.einsum(FORMS[axis], vectors, field, precision=HIGH))
    return result

def residual_of(field, own, ghosts, mask, penalty, tables):
    stiffness = tables[2]
    total = -(jnp.einsum('il,ljke->ijke', stiffness, field, precision=HIGH) + jnp.einsum('jl,ilke->ijke', stiffness, field, precision=HIGH) + jnp.einsum('kl,ijle->ijke', stiffness, field, precision=HIGH))
    for face in range(6):
        axis = face // 2
        side = face % 2
        sign = 2.0 * side - 1.0
        jump = own[face][0] - ghosts[face][0]
        mean_slope = 0.5 * (own[face][1] + ghosts[face][1])
        face_terms = jnp.stack([sign * mean_slope - penalty * jump, 0.5 * sign * jump])
        vectors = jnp.stack([tables[3][side], tables[4][side]])
        total = total + jnp.einsum(ADDS[axis], vectors, face_terms, precision=HIGH)
    return mask * total

def neighbour_ids(face_link, send_index):
    devices = N_WIDE * N_NARROW
    ranks = jnp.arange(ELEMS, dtype=jnp.int32) // ELEM_DEV
    sources = ((-N_NARROW, 1), (N_NARROW, 0), (0, -1), (0, -1), (-1, 3), (1, 2))
    result = []
    for face in range(6):
        link = face_link[face]
        local_ids = ranks * ELEM_DEV + link
        offset, row = sources[face]
        if row < 0:
            result.append(jnp.where(link < 0, -1, local_ids).astype(jnp.int32))
            continue
        source = jnp.clip(ranks + offset, 0, devices - 1)
        slot = jnp.clip(link - ELEM_DEV, 0, SLOTS - 1)
        remote = source * ELEM_DEV + send_index[row, source * SLOTS + slot]
        chosen = jnp.where(link >= ELEM_DEV, remote, local_ids)
        result.append(jnp.where(link < 0, -1, chosen).astype(jnp.int32))
    return result

def section(field, mask, penalty, neighbours, tables):
    transformed = kirchhoff(field, mask, tables)
    own = face_traces(transformed, tables)
    ghosts = []
    for face in range(6):
        targets = neighbours[face]
        gathered = jnp.take(own[face ^ 1], jnp.maximum(targets, 0), axis=3)
        mirror = jnp.stack([-own[face][0], own[face][1]])
        ghosts.append(jnp.where(targets[None, None, None, :] < 0, mirror, gathered))
    return residual_of(transformed, own, ghosts, mask, penalty, tables)

def reference(coefficients, degree, new_degree, face_link, send_index, new_owner):
    tables = basis_tables(MODES, QUAD)
    mask = degree_mask(degree, MODES)
    penalty = ((degree + 1) ** 2).astype(jnp.float32)
    neighbours = neighbour_ids(face_link, send_index)
    start = coefficients * mask
    first = start + STEP_SIZE * section(start, mask, penalty, neighbours, tables)
    second = 0.5 * (start + first + STEP_SIZE * section(first, mask, penalty, neighbours, tables))
    kept = second * degree_mask(new_degree, MODES)
    devices = N_WIDE * N_NARROW
    target = new_owner[:, 0]
    onehot = (target[:, None] == jnp.arange(devices, dtype=jnp.int32)[None, :]).astype(jnp.int32)
    blocks = onehot.reshape(devices, ELEM_DEV, devices)
    before = jnp.cumsum(blocks, axis=1) - blocks
    rank = lax.optimization_barrier(jnp.sum(before * blocks, axis=2)).reshape(ELEMS)
    source = jnp.arange(ELEMS, dtype=jnp.int32) // ELEM_DEV
    column = target * (devices * CAPR) + source * CAPR + rank
    moved = jnp.zeros((MODES, MODES, MODES, devices * devices * CAPR), jnp.float32)
    return moved.at[:, :, :, column].set(kept)
```

```python
import functools

import jax
import jax.numpy as jnp
import numpy as np
from jax import lax
from jax.experimental import pallas as pl
from jax.experimental.pallas import tpu as pltpu
from jax.sharding import PartitionSpec as P

MODES = 7
QUAD = 8
SIDE = 8
DEPTH = 16
LANES = 128
ROWS = 352
FACE = 56
PAIR = 2 * FACE
TRACE = 6 * PAIR
WORK = 256
STEP_SIZE = 0.0003
MESH = pl.DeviceIdType.MESH
F32 = jnp.float32
BF16 = jnp.bfloat16


def legendre_rows(points, count):
    values = [points * 0.0 + 1.0, points.copy()]
    slopes = [points * 0.0, points * 0.0 + 1.0]
    for order in range(1, count):
        values.append(
            ((2.0 * order + 1.0) * points * values[order] - order * values[order - 1])
            / (order + 1.0)
        )
        slopes.append(slopes[order - 1] + (2.0 * order + 1.0) * values[order])
    return (np.stack(values[: count + 1]), np.stack(slopes[: count + 1]))


def gauss_rule(count):
    points = np.cos(np.pi * (np.arange(count) + 0.75) / (count + 0.5))
    for sweep in range(60):
        values, slopes = legendre_rows(points, count)
        points = points - values[count] / slopes[count]
    values, slopes = legendre_rows(points, count)
    weights = 2.0 / ((1.0 - points * points) * slopes[count] ** 2)
    return (points[::-1], weights[::-1])


def operators():
    points, weights = gauss_rule(QUAD)
    scales = np.sqrt((2.0 * np.arange(MODES) + 1.0) / 2.0)
    value_rows, slope_rows = legendre_rows(points, MODES)
    values = value_rows[:MODES].T * scales
    slopes = slope_rows[:MODES].T * scales
    stiffness = slopes.T @ (weights[:, None] * slopes)
    project = (values * weights[:, None]).T
    orders = np.arange(MODES)
    ends = np.stack([(-1.0) ** orders, np.ones(MODES)]) * scales
    end_slopes = (
        np.stack([(-1.0) ** (orders + 1), np.ones(MODES)]) * (orders * (orders + 1) / 2.0) * scales
    )
    eye = np.eye(MODES)

    def kron(first, second, third):
        return np.kron(first, np.kron(second, third))

    modes = MODES**3
    evaluate = np.zeros((QUAD**3, ROWS))
    evaluate[:, :modes] = kron(values, values, values)
    back = np.zeros((ROWS, QUAD**3))
    back[:modes] = kron(project, project, project)
    trace = np.zeros((TRACE, ROWS))
    plane = MODES**2
    for face in range(6):
        axis, side = divmod(face, 2)
        for kind, vector in enumerate((ends[side], end_slopes[side])):
            parts = [eye, eye, eye]
            parts[axis] = vector[None, :]
            base = face * PAIR + kind * FACE
            trace[base : base + plane, :modes] = kron(*parts)
    inner = kron(stiffness, eye, eye) + kron(eye, stiffness, eye) + kron(eye, eye, stiffness)
    gather = np.zeros((ROWS, TRACE + ROWS))
    gather[:, :TRACE] = trace.T
    gather[:modes, TRACE : TRACE + modes] = -inner
    return evaluate, back, trace, gather


def host_halves(array):
    high = array.astype(jnp.bfloat16)
    low = (array - high.astype(np.float64)).astype(jnp.bfloat16)
    return jnp.stack([jnp.asarray(high), jnp.asarray(low)])


def highest_modes():
    order = np.arange(MODES)
    top = np.maximum(np.maximum(order[:, None, None], order[None, :, None]), order[None, None, :])
    column = np.full((ROWS, LANES), 99, np.int32)
    column[: MODES**3] = top.reshape(-1)[:, None]
    return jnp.asarray(column)


def split(array):
    high = array.astype(BF16)
    return high, (array - high.astype(F32)).astype(BF16)


def product(table_ref, high, low):
    def dot(left, right):
        return jnp.dot(left, right, preferred_element_type=F32)

    return dot(table_ref[0], high) + (dot(table_ref[0], low) + dot(table_ref[1], high))


def take(table, index):
    row, lane = index >> 7, index & (LANES - 1)
    result = jnp.zeros_like(table)
    for s in range(table.shape[0]):
        line = jnp.broadcast_to(table[s : s + 1, :], table.shape)
        result = jnp.where(row == s, jnp.take_along_axis(line, lane, axis=1), result)
    return result


def arrange(
    devices, capacity, coef_ref, degree_ref, new_degree_ref, link_ref, owner_ref, top_ref,
    start_ref, aux_ref, flat_ref, pair_ref,
):
    rows = SIDE
    count = rows * LANES
    iota = lax.broadcasted_iota
    sub, lane = iota(jnp.int32, (rows, LANES), 0), iota(jnp.int32, (rows, LANES), 1)
    own = sub * LANES + lane
    links = [
        jnp.concatenate(
            [link_ref[face : face + 1, b * LANES : (b + 1) * LANES] for b in range(rows)], axis=0
        )
        for face in range(6)
    ]
    inside = [(link >= 0) & (link < count) for link in links]
    corner = ~(inside[0] | inside[2] | inside[4])
    first = jnp.sum(jnp.where(corner, own, 0).astype(F32), axis=1, keepdims=True)
    first = jnp.sum(first, axis=0, keepdims=True).astype(jnp.int32)
    order = jnp.broadcast_to(first, (rows, LANES))
    for face, place, bits in ((3, lane & (DEPTH - 1), 4), (5, lane >> 4, 3), (1, sub, 3)):
        step = jnp.where(inside[face], links[face], own)
        for bit in range(bits):
            order = jnp.where(((place >> bit) & 1) == 1, take(step, order), order)
            if bit < bits - 1:
                step = take(step, step)
    owner = owner_ref[...]
    before = (iota(jnp.int32, (LANES, LANES), 0) < iota(jnp.int32, (LANES, LANES), 1)).astype(F32)
    before = before.astype(BF16)
    base = jnp.zeros((devices, 1), F32)
    lines = []
    for b in range(rows):
        named = (iota(jnp.int32, (devices, LANES), 0) == owner[b : b + 1, :]).astype(F32)
        earlier = jnp.dot(named.astype(BF16), before, preferred_element_type=F32) + base
        lines.append(jnp.sum(named * earlier, axis=0, keepdims=True))
        base = base + jnp.sum(named, axis=1, keepdims=True)
    rank = jnp.concatenate(lines, axis=0).astype(jnp.int32)
    column = take(owner * capacity + rank, order)
    degree = take(degree_ref[...], order)
    new_degree = take(new_degree_ref[...], order)
    aux_ref[...] = jnp.zeros_like(aux_ref)
    for b in range(rows):
        at = slice(b * LANES, (b + 1) * LANES)
        for row, array in enumerate((degree, new_degree, column, order)):
            aux_ref[row : row + 1, at] = array[b : b + 1, :]
    flat_ref[ROWS - 16 :, :] = jnp.zeros((16, count), F32)
    for i in range(MODES):
        for j in range(MODES):
            at = (i * MODES + j) * MODES
            flat_ref[at : at + MODES, :] = coef_ref[i, j]
    high, low = split(flat_ref[...])
    pair_ref[:ROWS, :] = high
    pair_ref[ROWS:, :] = low
    top = top_ref[:, :1]

    def body(c, carry):
        at = pl.ds(pl.multiple_of(c * WORK, WORK), WORK)
        chooser = (iota(jnp.int32, (count, WORK), 0) == aux_ref[3:4, at]).astype(F32).astype(BF16)
        both = jnp.dot(pair_ref[...], chooser, preferred_element_type=F32)
        mask = top <= aux_ref[0:1, at]
        start_ref[:, at] = jnp.where(mask, both[:ROWS] + both[ROWS:], 0.0)
        return carry

    lax.fori_loop(0, count // WORK, body, 0)


def evolve(
    wide, narrow, capacity, start_ref, aux_ref, top_ref, eval_ref, back_ref, trace_ref, gather_ref,
    out_ref,
    state_ref, face_refs, up_ref, down_ref, high_ref, low_ref, pair_ref, send_ref,
    z_out, z_in, halo_send, halo_recv, send_sem, recv_sem, local_sem,
):
    devices = wide * narrow
    count = start_ref.shape[1]
    w, n = lax.axis_index("wide"), lax.axis_index("narrow")
    me = w * narrow + n
    barrier = pltpu.get_barrier_semaphore()

    def greet(k, carry):
        other = lax.rem(me + k, devices)
        pl.semaphore_signal(
            barrier, inc=1, device_id=(other // narrow, lax.rem(other, narrow)), device_id_type=MESH
        )
        return carry

    lax.fori_loop(1, devices, greet, 0)
    top = top_ref[:, :1]
    iota = lax.broadcasted_iota
    lane = iota(jnp.int32, (PAIR, LANES), 1)
    flip = jnp.where(iota(jnp.int32, (PAIR, LANES), 0) < FACE, -1.0, 1.0)

    def local_part(source_ref):
        def body(c, carry):
            at = pl.ds(pl.multiple_of(c * WORK, WORK), WORK)
            values = product(eval_ref, *split(source_ref[:, at]))
            values = values + values * values * values * (1.0 / 3.0)
            field = jnp.where(top <= aux_ref[0:1, at], product(back_ref, *split(values)), 0.0)
            high, low = split(field)
            high_ref[TRACE:, at] = high
            low_ref[TRACE:, at] = low
            traces = product(trace_ref, high, low)
            down_ref[:, at] = traces[:PAIR]
            up_ref[:, pl.ds(pl.multiple_of(c * WORK + LANES, LANES), WORK)] = traces[
                PAIR : 2 * PAIR
            ]
            for face in range(2, 6):
                face_refs[face - 2, :, at] = traces[face * PAIR : (face + 1) * PAIR]
            return carry

        lax.fori_loop(0, count // WORK, body, 0)

    def exchange(turn):
        low_side = jnp.zeros((PAIR, LANES), F32)
        high_side = jnp.zeros((PAIR, LANES), F32)
        for b in range(SIDE):
            at = slice(b * LANES, (b + 1) * LANES)
            mine = (lane >> 4) == b
            lower = face_refs[2, :, at]
            upper = face_refs[3, :, at]
            shift = b * DEPTH
            low_side = jnp.where(mine, pltpu.roll(lower, shift, 1) if shift else lower, low_side)
            shift = (b * DEPTH + DEPTH) % LANES
            high_side = jnp.where(mine, pltpu.roll(upper, shift, 1) if shift else upper, high_side)
        z_out[turn, 0] = low_side
        z_out[turn, 1] = high_side
        plans = (
            (w > 0, z_out.at[turn, 2], z_in.at[turn, 3], (w - 1, n)),
            (w < wide - 1, z_out.at[turn, 3], z_in.at[turn, 2], (w + 1, n)),
            (n > 0, z_out.at[turn, 0], z_in.at[turn, 1], (w, n - 1)),
            (n < narrow - 1, z_out.at[turn, 1], z_in.at[turn, 0], (w, n + 1)),
        )
        z_out[turn, 2] = down_ref[:, 0:LANES]
        z_out[turn, 3] = up_ref[:, count : count + LANES]
        into = (3, 2, 1, 0)
        side_of = (2, 3, 0, 1)

        def copy(k):
            return pltpu.make_async_remote_copy(
                src_ref=plans[k][1],
                dst_ref=plans[k][2],
                send_sem=halo_send.at[turn, k],
                recv_sem=halo_recv.at[turn, into[k]],
                device_id=plans[k][3],
                device_id_type=MESH,
            )

        for k in range(4):
            pl.when(plans[k][0])(lambda k=k: copy(k).start())

        def finish():
            for k in range(4):
                slot = side_of[k]

                def arrive(k=k, slot=slot):
                    pltpu.make_async_remote_copy(
                        src_ref=plans[k][1],
                        dst_ref=z_in.at[turn, slot],
                        send_sem=halo_send.at[turn, k],
                        recv_sem=halo_recv.at[turn, slot],
                        device_id=plans[k][3],
                        device_id_type=MESH,
                    ).wait()

                def mirror(slot=slot):
                    z_in[turn, slot] = z_out[turn, slot] * flip

                pl.when(plans[k][0])(arrive)
                pl.when(jnp.logical_not(plans[k][0]))(mirror)
            up_ref[:, 0:LANES] = z_in[turn, 2]
            down_ref[:, count : count + LANES] = z_in[turn, 3]

        return finish

    def terms(turn, b, faces):
        at = slice(b * LANES, (b + 1) * LANES)
        later = slice((b + 1) * LANES, (b + 2) * LANES)
        sigma = (aux_ref[0:1, at] + 1).astype(F32)
        sigma = sigma * sigma
        for face in faces:
            sign = 2.0 * (face % 2) - 1.0
            if face == 0:
                own, ghost = down_ref[:, at], up_ref[:, at]
            elif face == 1:
                own, ghost = up_ref[:, later], down_ref[:, later]
            else:
                own, other = face_refs[face - 2, :, at], face_refs[(face ^ 1) - 2, :, at]
                if face == 2:
                    edge, ghost = (lane & (DEPTH - 1)) == 0, pltpu.roll(other, 1, 1)
                    outer = own * flip
                elif face == 3:
                    edge, ghost = (lane & (DEPTH - 1)) == DEPTH - 1, pltpu.roll(other, LANES - 1, 1)
                    outer = own * flip
                elif face == 4:
                    edge, ghost = (lane >> 4) == 0, pltpu.roll(other, DEPTH, 1)
                    shift = (LANES - b * DEPTH) % LANES
                    outer = z_in[turn, 0]
                    outer = pltpu.roll(outer, shift, 1) if shift else outer
                else:
                    edge, ghost = (lane >> 4) == SIDE - 1, pltpu.roll(other, LANES - DEPTH, 1)
                    shift = (LANES - DEPTH - b * DEPTH) % LANES
                    outer = z_in[turn, 1]
                    outer = pltpu.roll(outer, shift, 1) if shift else outer
                ghost = jnp.where(edge, outer, ghost)
            jump = own[:FACE] - ghost[:FACE]
            sums = own[FACE:] + ghost[FACE:]
            base = face * PAIR
            both = jnp.concatenate(
                [(0.5 * sign) * sums - sigma * jump, (0.5 * sign) * jump], axis=0
            )
            high, low = split(both)
            high_ref[base : base + PAIR, at] = high
            low_ref[base : base + PAIR, at] = low

    def residual(c):
        at = pl.ds(pl.multiple_of(c * WORK, WORK), WORK)
        rate = product(gather_ref, high_ref[:, at], low_ref[:, at])
        return at, jnp.where(top <= aux_ref[0:1, at], rate, 0.0) * STEP_SIZE

    def section(turn, source_ref, before_send, store):
        local_part(source_ref)
        before_send()
        finish = exchange(turn)
        for b in range(SIDE):
            terms(turn, b, (2, 3))
        finish()
        for b in range(SIDE):
            terms(turn, b, (0, 1, 4, 5))
        lax.fori_loop(0, count // WORK, store, 0)

    def store_first(c, carry):
        at, change = residual(c)
        state_ref[:, at] = start_ref[:, at] + change
        return carry

    def store_second(c, carry):
        at, change = residual(c)
        second = 0.5 * (start_ref[:, at] + state_ref[:, at] + change)
        high, low = split(jnp.where(top <= aux_ref[1:2, at], second, 0.0))
        pair_ref[:ROWS, at] = high
        pair_ref[ROWS:, at] = low
        return carry

    section(0, start_ref, lambda: pl.semaphore_wait(barrier, devices - 1), store_first)
    section(1, state_ref, lambda: None, store_second)

    share = LANES // capacity
    height = send_ref.shape[1]
    tiles = devices * capacity // LANES
    first_tile = me // share
    wide_lane = iota(jnp.int32, (height, LANES), 1)

    def outgoing(other):
        return pltpu.make_async_remote_copy(
            src_ref=send_ref.at[other],
            dst_ref=out_ref.at[me],
            send_sem=send_sem.at[other],
            recv_sem=recv_sem.at[me],
            device_id=(other // narrow, lax.rem(other, narrow)),
            device_id_type=MESH,
        )

    def place(t, carry):
        tile = lax.rem(first_tile + t, tiles)
        slot = iota(jnp.int32, (LANES, count), 0) + tile * LANES
        chooser = (slot == aux_ref[2:3, :]).astype(F32).astype(BF16)
        both = lax.dot_general(
            pair_ref[...], chooser, (((1,), (1,)), ((), ())), preferred_element_type=F32
        )
        columns = both[:ROWS] + both[ROWS:]
        if share * height > ROWS:
            columns = jnp.concatenate(
                [columns, jnp.zeros((share * height - ROWS, LANES), F32)], axis=0
            )
        for j in range(share):
            block = jnp.zeros((height, LANES), F32)
            for q in range(share):
                piece = columns[q * height : (q + 1) * height]
                shift = ((q - j) * capacity) % LANES
                piece = pltpu.roll(piece, shift, 1) if shift else piece
                block = jnp.where(wide_lane // capacity == q, piece, block)
            other = tile * share + j
            send_ref[other] = block

            @pl.when(other != me)
            def _():
                outgoing(other).start()

        return carry

    lax.fori_loop(0, tiles, place, 0)
    own = pltpu.make_async_copy(send_ref.at[me], out_ref.at[me], local_sem)
    own.start()

    def collect(k, carry):
        source = lax.rem(me + devices - k, devices)
        pltpu.make_async_remote_copy(
            src_ref=send_ref.at[source],
            dst_ref=out_ref.at[source],
            send_sem=send_sem.at[source],
            recv_sem=recv_sem.at[source],
            device_id=(source // narrow, lax.rem(source, narrow)),
            device_id_type=MESH,
        ).wait()
        return carry

    lax.fori_loop(1, devices, collect, 0)
    own.wait()


def unpack(capacity, block_ref, moved_ref, flat_ref):
    share, height, _ = block_ref.shape
    lane = lax.broadcasted_iota(jnp.int32, (height, LANES), 1)
    for q in range(share):
        piece = jnp.zeros((height, LANES), F32)
        for j in range(share):
            shift = ((j - q) * capacity) % LANES
            block = block_ref[j]
            block = pltpu.roll(block, shift, 1) if shift else block
            piece = jnp.where(lane // capacity == j, block, piece)
        flat_ref[q * height : (q + 1) * height, :] = piece
    for i in range(MODES):
        for j in range(MODES):
            at = (i * MODES + j) * MODES
            moved_ref[i, j] = flat_ref[at : at + MODES, :]


def on_device(coefficients, degree, new_degree, face_link, send_index, new_owner):
    wide, narrow = lax.axis_size("wide"), lax.axis_size("narrow")
    devices = wide * narrow
    count = coefficients.shape[3]
    capacity = max(2, 2 * count // devices)
    share = LANES // capacity
    modes = MODES**3
    height = -(-(-(-modes // share)) // 8) * 8
    evaluate, back, trace, gather = (host_halves(array) for array in operators())
    top = highest_modes()
    vmem = pl.BlockSpec(memory_space=pltpu.VMEM)
    square = (SIDE, LANES)
    start, aux = pl.pallas_call(
        functools.partial(arrange, devices, capacity),
        out_shape=(
            jax.ShapeDtypeStruct((ROWS, count), F32),
            jax.ShapeDtypeStruct((8, count), jnp.int32),
        ),
        in_specs=[vmem] * 6,
        out_specs=(vmem, vmem),
        scratch_shapes=[pltpu.VMEM((ROWS, count), F32), pltpu.VMEM((2 * ROWS, count), BF16)],
        compiler_params=pltpu.CompilerParams(vmem_limit_bytes=48 * 2**20),
        name="arrange",
    )(
        coefficients,
        degree.reshape(square),
        new_degree.reshape(square),
        face_link,
        new_owner.reshape(square),
        top,
    )
    blocks = pl.pallas_call(
        functools.partial(evolve, wide, narrow, capacity),
        out_shape=jax.ShapeDtypeStruct((devices, height, LANES), F32),
        in_specs=[vmem] * 7,
        out_specs=pl.BlockSpec(memory_space=pl.ANY),
        scratch_shapes=[
            pltpu.VMEM((ROWS, count), F32),
            pltpu.VMEM((4, PAIR, count), F32),
            pltpu.VMEM((PAIR, count + LANES), F32),
            pltpu.VMEM((PAIR, count + LANES), F32),
            pltpu.VMEM((TRACE + ROWS, count), BF16),
            pltpu.VMEM((TRACE + ROWS, count), BF16),
            pltpu.VMEM((2 * ROWS, count), BF16),
            pltpu.VMEM((devices, height, LANES), F32),
            pltpu.VMEM((2, 4, PAIR, LANES), F32),
            pltpu.VMEM((2, 4, PAIR, LANES), F32),
            pltpu.SemaphoreType.DMA((2, 4)),
            pltpu.SemaphoreType.DMA((2, 4)),
            pltpu.SemaphoreType.DMA((devices,)),
            pltpu.SemaphoreType.DMA((devices,)),
            pltpu.SemaphoreType.DMA,
        ],
        compiler_params=pltpu.CompilerParams(
            collective_id=0, has_side_effects=True, vmem_limit_bytes=56 * 2**20
        ),
        name="evolve",
    )(start, aux, top, evaluate, back, trace, gather)
    return pl.pallas_call(
        functools.partial(unpack, capacity),
        grid=(devices // share,),
        out_shape=jax.ShapeDtypeStruct((MODES, MODES, MODES, devices * capacity), F32),
        in_specs=[pl.BlockSpec((share, height, LANES), lambda t: (t, 0, 0))],
        out_specs=pl.BlockSpec((MODES, MODES, MODES, LANES), lambda t: (0, 0, 0, t)),
        scratch_shapes=[pltpu.VMEM((share * height, LANES), F32)],
        compiler_params=pltpu.CompilerParams(vmem_limit_bytes=32 * 2**20),
        name="unpack",
    )(blocks)


def solution(mesh):
    placed = (
        P(None, None, None, ("wide", "narrow")),
        P(("wide", "narrow")),
        P(("wide", "narrow")),
        P(None, ("wide", "narrow")),
        P(None, ("wide", "narrow")),
        P(("wide", "narrow"), None),
    )
    return jax.shard_map(
        on_device,
        mesh=mesh,
        in_specs=placed,
        out_specs=P(None, None, None, ("wide", "narrow")),
        check_vma=False,
    )
```

```python
import functools

import jax
import jax.numpy as jnp
import numpy as np
from jax import lax
from jax.experimental import pallas as pl
from jax.experimental.pallas import tpu as pltpu
from jax.sharding import PartitionSpec as P

MODES = 7
QUAD = 8
SIDE = 8
DEPTH = 16
LANES = 128
ROWS = 352
FACE = 56
PAIR = 2 * FACE
TRACE = 6 * PAIR
WORK = 256
STEP_SIZE = 0.0003
MESH = pl.DeviceIdType.MESH
F32 = jnp.float32
BF16 = jnp.bfloat16


def legendre_rows(points, count):
    values = [points * 0.0 + 1.0, points.copy()]
    slopes = [points * 0.0, points * 0.0 + 1.0]
    for order in range(1, count):
        values.append(
            ((2.0 * order + 1.0) * points * values[order] - order * values[order - 1])
            / (order + 1.0)
        )
        slopes.append(slopes[order - 1] + (2.0 * order + 1.0) * values[order])
    return (np.stack(values[: count + 1]), np.stack(slopes[: count + 1]))


def gauss_rule(count):
    points = np.cos(np.pi * (np.arange(count) + 0.75) / (count + 0.5))
    for sweep in range(60):
        values, slopes = legendre_rows(points, count)
        points = points - values[count] / slopes[count]
    values, slopes = legendre_rows(points, count)
    weights = 2.0 / ((1.0 - points * points) * slopes[count] ** 2)
    return (points[::-1], weights[::-1])


def operators():
    points, weights = gauss_rule(QUAD)
    scales = np.sqrt((2.0 * np.arange(MODES) + 1.0) / 2.0)
    value_rows, slope_rows = legendre_rows(points, MODES)
    values = value_rows[:MODES].T * scales
    slopes = slope_rows[:MODES].T * scales
    stiffness = slopes.T @ (weights[:, None] * slopes)
    project = (values * weights[:, None]).T
    orders = np.arange(MODES)
    ends = np.stack([(-1.0) ** orders, np.ones(MODES)]) * scales
    end_slopes = (
        np.stack([(-1.0) ** (orders + 1), np.ones(MODES)]) * (orders * (orders + 1) / 2.0) * scales
    )
    eye = np.eye(MODES)

    def kron(first, second, third):
        return np.kron(first, np.kron(second, third))

    modes = MODES**3
    evaluate = np.zeros((QUAD**3, ROWS))
    evaluate[:, :modes] = kron(values, values, values)
    back = np.zeros((ROWS, QUAD**3))
    back[:modes] = kron(project, project, project)
    trace = np.zeros((TRACE, ROWS))
    plane = MODES**2
    for face in range(6):
        axis, side = divmod(face, 2)
        for kind, vector in enumerate((ends[side], end_slopes[side])):
            parts = [eye, eye, eye]
            parts[axis] = vector[None, :]
            base = face * PAIR + kind * FACE
            trace[base : base + plane, :modes] = kron(*parts)
    inner = kron(stiffness, eye, eye) + kron(eye, stiffness, eye) + kron(eye, eye, stiffness)
    gather = np.zeros((ROWS, TRACE + ROWS))
    gather[:, :TRACE] = trace.T
    gather[:modes, TRACE : TRACE + modes] = -inner
    return evaluate, back, trace, gather


def host_halves(array):
    high = array.astype(jnp.bfloat16)
    low = (array - high.astype(np.float64)).astype(jnp.bfloat16)
    return jnp.stack([jnp.asarray(high), jnp.asarray(low)])


def highest_modes():
    order = np.arange(MODES)
    top = np.maximum(np.maximum(order[:, None, None], order[None, :, None]), order[None, None, :])
    column = np.full((ROWS, LANES), 99, np.int32)
    column[: MODES**3] = top.reshape(-1)[:, None]
    return jnp.asarray(column)


def split(array):
    high = array.astype(BF16)
    return high, (array - high.astype(F32)).astype(BF16)


def product(table_ref, high, low):
    def dot(left, right):
        return jnp.dot(left, right, preferred_element_type=F32)

    return dot(table_ref[0], high) + (dot(table_ref[0], low) + dot(table_ref[1], high))


def take(table, index):
    row, lane = index >> 7, index & (LANES - 1)
    result = jnp.zeros_like(table)
    for s in range(table.shape[0]):
        line = jnp.broadcast_to(table[s : s + 1, :], table.shape)
        result = jnp.where(row == s, jnp.take_along_axis(line, lane, axis=1), result)
    return result


def arrange(
    devices, capacity, coef_ref, degree_ref, new_degree_ref, link_ref, owner_ref, top_ref,
    start_ref, aux_ref, flat_ref, pair_ref,
):
    rows = SIDE
    count = rows * LANES
    iota = lax.broadcasted_iota
    sub, lane = iota(jnp.int32, (rows, LANES), 0), iota(jnp.int32, (rows, LANES), 1)
    own = sub * LANES + lane
    links = [
        jnp.concatenate(
            [link_ref[face : face + 1, b * LANES : (b + 1) * LANES] for b in range(rows)], axis=0
        )
        for face in range(6)
    ]
    inside = [(link >= 0) & (link < count) for link in links]
    corner = ~(inside[0] | inside[2] | inside[4])
    first = jnp.sum(jnp.where(corner, own, 0).astype(F32), axis=1, keepdims=True)
    first = jnp.sum(first, axis=0, keepdims=True).astype(jnp.int32)
    order = jnp.broadcast_to(first, (rows, LANES))
    for face, place, bits in ((3, lane & (DEPTH - 1), 4), (5, lane >> 4, 3), (1, sub, 3)):
        step = jnp.where(inside[face], links[face], own)
        for bit in range(bits):
            order = jnp.where(((place >> bit) & 1) == 1, take(step, order), order)
            if bit < bits - 1:
                step = take(step, step)
    owner = owner_ref[...]
    before = (iota(jnp.int32, (LANES, LANES), 0) < iota(jnp.int32, (LANES, LANES), 1)).astype(F32)
    before = before.astype(BF16)
    base = jnp.zeros((devices, 1), F32)
    lines = []
    for b in range(rows):
        named = (iota(jnp.int32, (devices, LANES), 0) == owner[b : b + 1, :]).astype(F32)
        earlier = jnp.dot(named.astype(BF16), before, preferred_element_type=F32) + base
        lines.append(jnp.sum(named * earlier, axis=0, keepdims=True))
        base = base + jnp.sum(named, axis=1, keepdims=True)
    rank = jnp.concatenate(lines, axis=0).astype(jnp.int32)
    column = take(owner * capacity + rank, order)
    degree = take(degree_ref[...], order)
    new_degree = take(new_degree_ref[...], order)
    aux_ref[...] = jnp.zeros_like(aux_ref)
    for b in range(rows):
        at = slice(b * LANES, (b + 1) * LANES)
        for row, array in enumerate((degree, new_degree, column, order)):
            aux_ref[row : row + 1, at] = array[b : b + 1, :]
    flat_ref[ROWS - 16 :, :] = jnp.zeros((16, count), F32)
    for i in range(MODES):
        for j in range(MODES):
            at = (i * MODES + j) * MODES
            flat_ref[at : at + MODES, :] = coef_ref[i, j]
    high, low = split(flat_ref[...])
    pair_ref[:ROWS, :] = high
    pair_ref[ROWS:, :] = low
    top = top_ref[:, :1]

    def body(c, carry):
        at = pl.ds(pl.multiple_of(c * WORK, WORK), WORK)
        chooser = (iota(jnp.int32, (count, WORK), 0) == aux_ref[3:4, at]).astype(F32).astype(BF16)
        both = jnp.dot(pair_ref[...], chooser, preferred_element_type=F32)
        mask = top <= aux_ref[0:1, at]
        start_ref[:, at] = jnp.where(mask, both[:ROWS] + both[ROWS:], 0.0)
        return carry

    lax.fori_loop(0, count // WORK, body, 0)


def evolve(
    wide, narrow, capacity, aux_ref, top_ref, start_at, eval_at, back_at, trace_at, gather_at,
    moved_ref,
    start_ref, eval_ref, back_ref, trace_ref, gather_ref, table_sem, recv_ref, flat_ref, state_ref, face_refs, up_ref, down_ref, high_ref, low_ref, pair_ref, send_ref,
    z_out, z_in, halo_send, halo_recv, send_sem, recv_sem,
):
    devices = wide * narrow
    count = start_ref.shape[1]
    w, n = lax.axis_index("wide"), lax.axis_index("narrow")
    me = w * narrow + n
    barrier = pltpu.get_barrier_semaphore()
    pairs = ((start_at, start_ref), (eval_at, eval_ref), (back_at, back_ref))
    pairs = pairs + ((trace_at, trace_ref), (gather_at, gather_ref))
    loads = [
        pltpu.make_async_copy(source, target, table_sem.at[i])
        for i, (source, target) in enumerate(pairs)
    ]
    for load in loads:
        load.start()

    def greet(k, carry):
        other = lax.rem(me + k, devices)
        pl.semaphore_signal(
            barrier, inc=1, device_id=(other // narrow, lax.rem(other, narrow)), device_id_type=MESH
        )
        return carry

    lax.fori_loop(1, devices, greet, 0)
    top = top_ref[:, :1]
    iota = lax.broadcasted_iota
    lane = iota(jnp.int32, (PAIR, LANES), 1)
    flip = jnp.where(iota(jnp.int32, (PAIR, LANES), 0) < FACE, -1.0, 1.0)

    def local_part(source_ref):
        def body(c, carry):
            at = pl.ds(pl.multiple_of(c * WORK, WORK), WORK)
            values = product(eval_ref, *split(source_ref[:, at]))
            values = values + values * values * values * (1.0 / 3.0)
            field = jnp.where(top <= aux_ref[0:1, at], product(back_ref, *split(values)), 0.0)
            high, low = split(field)
            high_ref[TRACE:, at] = high
            low_ref[TRACE:, at] = low
            traces = product(trace_ref, high, low)
            down_ref[:, at] = traces[:PAIR]
            up_ref[:, pl.ds(pl.multiple_of(c * WORK + LANES, LANES), WORK)] = traces[
                PAIR : 2 * PAIR
            ]
            for face in range(2, 6):
                face_refs[face - 2, :, at] = traces[face * PAIR : (face + 1) * PAIR]
            return carry

        lax.fori_loop(0, count // WORK, body, 0)

    def exchange(turn):
        low_side = jnp.zeros((PAIR, LANES), F32)
        high_side = jnp.zeros((PAIR, LANES), F32)
        for b in range(SIDE):
            at = slice(b * LANES, (b + 1) * LANES)
            mine = (lane >> 4) == b
            lower = face_refs[2, :, at]
            upper = face_refs[3, :, at]
            shift = b * DEPTH
            low_side = jnp.where(mine, pltpu.roll(lower, shift, 1) if shift else lower, low_side)
            shift = (b * DEPTH + DEPTH) % LANES
            high_side = jnp.where(mine, pltpu.roll(upper, shift, 1) if shift else upper, high_side)
        z_out[turn, 0] = low_side
        z_out[turn, 1] = high_side
        plans = (
            (w > 0, z_out.at[turn, 2], z_in.at[turn, 3], (w - 1, n)),
            (w < wide - 1, z_out.at[turn, 3], z_in.at[turn, 2], (w + 1, n)),
            (n > 0, z_out.at[turn, 0], z_in.at[turn, 1], (w, n - 1)),
            (n < narrow - 1, z_out.at[turn, 1], z_in.at[turn, 0], (w, n + 1)),
        )
        z_out[turn, 2] = down_ref[:, 0:LANES]
        z_out[turn, 3] = up_ref[:, count : count + LANES]
        into = (3, 2, 1, 0)
        side_of = (2, 3, 0, 1)

        def copy(k):
            return pltpu.make_async_remote_copy(
                src_ref=plans[k][1],
                dst_ref=plans[k][2],
                send_sem=halo_send.at[turn, k],
                recv_sem=halo_recv.at[turn, into[k]],
                device_id=plans[k][3],
                device_id_type=MESH,
            )

        for k in range(4):
            pl.when(plans[k][0])(lambda k=k: copy(k).start())

        def finish():
            for k in range(4):
                slot = side_of[k]

                def arrive(k=k, slot=slot):
                    pltpu.make_async_remote_copy(
                        src_ref=plans[k][1],
                        dst_ref=z_in.at[turn, slot],
                        send_sem=halo_send.at[turn, k],
                        recv_sem=halo_recv.at[turn, slot],
                        device_id=plans[k][3],
                        device_id_type=MESH,
                    ).wait()

                def mirror(slot=slot):
                    z_in[turn, slot] = z_out[turn, slot] * flip

                pl.when(plans[k][0])(arrive)
                pl.when(jnp.logical_not(plans[k][0]))(mirror)
            up_ref[:, 0:LANES] = z_in[turn, 2]
            down_ref[:, count : count + LANES] = z_in[turn, 3]

        return finish

    def terms(turn, b, faces):
        at = slice(b * LANES, (b + 1) * LANES)
        later = slice((b + 1) * LANES, (b + 2) * LANES)
        sigma = (aux_ref[0:1, at] + 1).astype(F32)
        sigma = sigma * sigma
        for face in faces:
            sign = 2.0 * (face % 2) - 1.0
            if face == 0:
                own, ghost = down_ref[:, at], up_ref[:, at]
            elif face == 1:
                own, ghost = up_ref[:, later], down_ref[:, later]
            else:
                own, other = face_refs[face - 2, :, at], face_refs[(face ^ 1) - 2, :, at]
                if face == 2:
                    edge, ghost = (lane & (DEPTH - 1)) == 0, pltpu.roll(other, 1, 1)
                    outer = own * flip
                elif face == 3:
                    edge, ghost = (lane & (DEPTH - 1)) == DEPTH - 1, pltpu.roll(other, LANES - 1, 1)
                    outer = own * flip
                elif face == 4:
                    edge, ghost = (lane >> 4) == 0, pltpu.roll(other, DEPTH, 1)
                    shift = (LANES - b * DEPTH) % LANES
                    outer = z_in[turn, 0]
                    outer = pltpu.roll(outer, shift, 1) if shift else outer
                else:
                    edge, ghost = (lane >> 4) == SIDE - 1, pltpu.roll(other, LANES - DEPTH, 1)
                    shift = (LANES - DEPTH - b * DEPTH) % LANES
                    outer = z_in[turn, 1]
                    outer = pltpu.roll(outer, shift, 1) if shift else outer
                ghost = jnp.where(edge, outer, ghost)
            jump = own[:FACE] - ghost[:FACE]
            sums = own[FACE:] + ghost[FACE:]
            base = face * PAIR
            both = jnp.concatenate(
                [(0.5 * sign) * sums - sigma * jump, (0.5 * sign) * jump], axis=0
            )
            high, low = split(both)
            high_ref[base : base + PAIR, at] = high
            low_ref[base : base + PAIR, at] = low

    def residual(c):
        at = pl.ds(pl.multiple_of(c * WORK, WORK), WORK)
        rate = product(gather_ref, high_ref[:, at], low_ref[:, at])
        return at, jnp.where(top <= aux_ref[0:1, at], rate, 0.0) * STEP_SIZE

    def section(turn, source_ref, before_send, store):
        local_part(source_ref)
        before_send()
        finish = exchange(turn)
        for b in range(SIDE):
            terms(turn, b, (2, 3))
        finish()
        for b in range(SIDE):
            terms(turn, b, (0, 1, 4, 5))
        lax.fori_loop(0, count // WORK, store, 0)

    def enter():
        loads[4].wait()
        pl.semaphore_wait(barrier, devices - 1)

    def store_first(c, carry):
        at, change = residual(c)
        state_ref[:, at] = start_ref[:, at] + change
        return carry

    def store_second(c, carry):
        at, change = residual(c)
        second = 0.5 * (start_ref[:, at] + state_ref[:, at] + change)
        high, low = split(jnp.where(top <= aux_ref[1:2, at], second, 0.0))
        pair_ref[:ROWS, at] = high
        pair_ref[ROWS:, at] = low
        return carry

    for load in loads[:4]:
        load.wait()
    section(0, start_ref, enter, store_first)
    section(1, state_ref, lambda: None, store_second)

    share = LANES // capacity
    height = send_ref.shape[1]
    tiles = devices * capacity // LANES
    first_tile = me // share + 1
    wide_lane = iota(jnp.int32, (height, LANES), 1)

    def outgoing(other):
        return pltpu.make_async_remote_copy(
            src_ref=send_ref.at[other],
            dst_ref=recv_ref.at[me],
            send_sem=send_sem.at[other],
            recv_sem=recv_sem.at[me],
            device_id=(other // narrow, lax.rem(other, narrow)),
            device_id_type=MESH,
        )

    def place(t, carry):
        tile = lax.rem(first_tile + t, tiles)
        slot = iota(jnp.int32, (LANES, count), 0) + tile * LANES
        chooser = (slot == aux_ref[2:3, :]).astype(F32).astype(BF16)
        both = lax.dot_general(
            pair_ref[...], chooser, (((1,), (1,)), ((), ())), preferred_element_type=F32
        )
        columns = both[:ROWS] + both[ROWS:]
        if share * height > ROWS:
            columns = jnp.concatenate(
                [columns, jnp.zeros((share * height - ROWS, LANES), F32)], axis=0
            )
        for j in range(share):
            block = jnp.zeros((height, LANES), F32)
            for q in range(share):
                piece = columns[q * height : (q + 1) * height]
                shift = ((q - j) * capacity) % LANES
                piece = pltpu.roll(piece, shift, 1) if shift else piece
                block = jnp.where(wide_lane // capacity == q, piece, block)
            other = tile * share + j

            @pl.when(other == me)
            def _(block=block):
                recv_ref[me] = block

            @pl.when(other != me)
            def _(block=block, other=other):
                send_ref[other] = block
                outgoing(other).start()

        return carry

    lax.fori_loop(0, tiles, place, 0)

    def collect(t, carry):
        tile = lax.rem(first_tile + tiles - t, tiles)
        pieces = [jnp.zeros((height, LANES), F32) for _ in range(share)]
        for j in range(share):
            source = tile * share + j

            @pl.when(source != me)
            def _(source=source):
                pltpu.make_async_remote_copy(
                    src_ref=send_ref.at[source],
                    dst_ref=recv_ref.at[source],
                    send_sem=send_sem.at[source],
                    recv_sem=recv_sem.at[source],
                    device_id=(source // narrow, lax.rem(source, narrow)),
                    device_id_type=MESH,
                ).wait()

            block = recv_ref[source]
            for q in range(share):
                shift = ((j - q) * capacity) % LANES
                moved = pltpu.roll(block, shift, 1) if shift else block
                pieces[q] = jnp.where(wide_lane // capacity == j, moved, pieces[q])
        for q in range(share):
            flat_ref[q * height : (q + 1) * height, :] = pieces[q]
        at = pl.ds(pl.multiple_of(tile * LANES, LANES), LANES)
        for i in range(MODES):
            for j in range(MODES):
                row = (i * MODES + j) * MODES
                moved_ref[i, j, :, at] = flat_ref[row : row + MODES, :]
        return carry

    lax.fori_loop(0, tiles, collect, 0)


def on_device(coefficients, degree, new_degree, face_link, send_index, new_owner):
    wide, narrow = lax.axis_size("wide"), lax.axis_size("narrow")
    devices = wide * narrow
    count = coefficients.shape[3]
    capacity = max(2, 2 * count // devices)
    share = LANES // capacity
    modes = MODES**3
    height = -(-(-(-modes // share)) // 8) * 8
    evaluate, back, trace, gather = (host_halves(array) for array in operators())
    top = highest_modes()
    vmem = pl.BlockSpec(memory_space=pltpu.VMEM)
    square = (SIDE, LANES)
    start, aux = pl.pallas_call(
        functools.partial(arrange, devices, capacity),
        out_shape=(
            jax.ShapeDtypeStruct((ROWS, count), F32),
            jax.ShapeDtypeStruct((8, count), jnp.int32),
        ),
        in_specs=[vmem] * 6,
        out_specs=(vmem, vmem),
        scratch_shapes=[pltpu.VMEM((ROWS, count), F32), pltpu.VMEM((2 * ROWS, count), BF16)],
        compiler_params=pltpu.CompilerParams(vmem_limit_bytes=48 * 2**20),
        name="arrange",
    )(
        coefficients,
        degree.reshape(square),
        new_degree.reshape(square),
        face_link,
        new_owner.reshape(square),
        top,
    )
    anywhere = pl.BlockSpec(memory_space=pl.ANY)
    return pl.pallas_call(
        functools.partial(evolve, wide, narrow, capacity),
        out_shape=jax.ShapeDtypeStruct((MODES, MODES, MODES, devices * capacity), F32),
        in_specs=[vmem] * 2 + [anywhere] * 5,
        out_specs=vmem,
        scratch_shapes=[
            pltpu.VMEM((ROWS, count), F32),
            pltpu.VMEM(evaluate.shape, BF16),
            pltpu.VMEM(back.shape, BF16),
            pltpu.VMEM(trace.shape, BF16),
            pltpu.VMEM(gather.shape, BF16),
            pltpu.SemaphoreType.DMA((5,)),
            pltpu.VMEM((devices, height, LANES), F32),
            pltpu.VMEM((share * height, LANES), F32),
            pltpu.VMEM((ROWS, count), F32),
            pltpu.VMEM((4, PAIR, count), F32),
            pltpu.VMEM((PAIR, count + LANES), F32),
            pltpu.VMEM((PAIR, count + LANES), F32),
            pltpu.VMEM((TRACE + ROWS, count), BF16),
            pltpu.VMEM((TRACE + ROWS, count), BF16),
            pltpu.VMEM((2 * ROWS, count), BF16),
            pltpu.VMEM((devices, height, LANES), F32),
            pltpu.VMEM((2, 4, PAIR, LANES), F32),
            pltpu.VMEM((2, 4, PAIR, LANES), F32),
            pltpu.SemaphoreType.DMA((2, 4)),
            pltpu.SemaphoreType.DMA((2, 4)),
            pltpu.SemaphoreType.DMA((devices,)),
            pltpu.SemaphoreType.DMA((devices,)),
        ],
        compiler_params=pltpu.CompilerParams(
            collective_id=0, has_side_effects=True, vmem_limit_bytes=36 * 2**20
        ),
        name="evolve",
    )(aux, top, start, evaluate, back, trace, gather)


def solution(mesh):
    placed = (
        P(None, None, None, ("wide", "narrow")),
        P(("wide", "narrow")),
        P(("wide", "narrow")),
        P(None, ("wide", "narrow")),
        P(None, ("wide", "narrow")),
        P(("wide", "narrow"), None),
    )
    return jax.shard_map(
        on_device,
        mesh=mesh,
        in_specs=placed,
        out_specs=P(None, None, None, ("wide", "narrow")),
        check_vma=False,
    )
```

```python
import functools

import jax
import jax.numpy as jnp
import numpy as np
from jax import lax
from jax.experimental import pallas as pl
from jax.experimental.pallas import tpu as pltpu
from jax.sharding import PartitionSpec as P

MODES = 7
QUAD = 8
SIDE = 8
DEPTH = 16
LANES = 128
ROWS = 352
FACE = 56
PAIR = 2 * FACE
TRACE = 6 * PAIR
WORK = 256
STEP_SIZE = 0.0003
MESH = pl.DeviceIdType.MESH
F32 = jnp.float32
BF16 = jnp.bfloat16


def legendre_rows(points, count):
    values = [points * 0.0 + 1.0, points.copy()]
    slopes = [points * 0.0, points * 0.0 + 1.0]
    for order in range(1, count):
        values.append(
            ((2.0 * order + 1.0) * points * values[order] - order * values[order - 1])
            / (order + 1.0)
        )
        slopes.append(slopes[order - 1] + (2.0 * order + 1.0) * values[order])
    return (np.stack(values[: count + 1]), np.stack(slopes[: count + 1]))


def gauss_rule(count):
    points = np.cos(np.pi * (np.arange(count) + 0.75) / (count + 0.5))
    for sweep in range(60):
        values, slopes = legendre_rows(points, count)
        points = points - values[count] / slopes[count]
    values, slopes = legendre_rows(points, count)
    weights = 2.0 / ((1.0 - points * points) * slopes[count] ** 2)
    return (points[::-1], weights[::-1])


def operators():
    points, weights = gauss_rule(QUAD)
    scales = np.sqrt((2.0 * np.arange(MODES) + 1.0) / 2.0)
    value_rows, slope_rows = legendre_rows(points, MODES)
    values = value_rows[:MODES].T * scales
    slopes = slope_rows[:MODES].T * scales
    stiffness = slopes.T @ (weights[:, None] * slopes)
    project = (values * weights[:, None]).T
    orders = np.arange(MODES)
    ends = np.stack([(-1.0) ** orders, np.ones(MODES)]) * scales
    end_slopes = (
        np.stack([(-1.0) ** (orders + 1), np.ones(MODES)]) * (orders * (orders + 1) / 2.0) * scales
    )
    eye = np.eye(MODES)
    scaled = np.ones(ROWS)
    scaled[: MODES**3] = np.kron(scales, np.kron(scales, scales))

    def kron(first, second, third):
        return np.kron(first, np.kron(second, third))

    modes = MODES**3
    evaluate = np.zeros((QUAD**3, ROWS))
    evaluate[:, :modes] = kron(values, values, values)
    back = np.zeros((ROWS, QUAD**3))
    back[:modes] = kron(project, project, project)
    back = back * scaled[:, None]
    gather = np.zeros((ROWS, TRACE + ROWS))
    trace = np.zeros((TRACE, ROWS))
    plane = MODES**2
    for face in range(6):
        axis, side = divmod(face, 2)
        for kind, vector in enumerate((ends[side], end_slopes[side])):
            parts = [eye, eye, eye]
            parts[axis] = (vector / scales)[None, :]
            base = face * PAIR + kind * FACE
            trace[base : base + plane, :modes] = kron(*parts)
            parts[axis] = (vector * scales / (1.0, 3.0)[kind])[:, None]
            gather[:modes, base : base + plane] = kron(*parts)
    inner = kron(stiffness, eye, eye) + kron(eye, stiffness, eye) + kron(eye, eye, stiffness)
    diagonal = np.zeros(ROWS)
    diagonal[:modes] = -np.diag(inner)
    ratio = scaled[:modes, None] / scaled[None, :modes]
    gather[:modes, TRACE : TRACE + modes] = (np.diag(np.diag(inner)) - inner) * ratio
    rates = STEP_SIZE * np.stack([1.0 / scaled, diagonal / scaled])
    rates = np.repeat(rates[:, :, None], LANES, axis=2).astype(np.float32)
    return thrice(evaluate), thrice(back), twice(trace), twice(gather), jnp.asarray(rates)


def thrice(array):
    high = array.astype(jnp.bfloat16)
    low = (array - high.astype(np.float64)).astype(jnp.bfloat16)
    return jnp.asarray(np.concatenate([high, high, low], axis=1))


def twice(array):
    high = array.astype(jnp.bfloat16)
    assert np.abs(high.astype(np.float64) - array).max() < 1e-9
    return jnp.asarray(np.concatenate([high, high], axis=1))


def highest_modes():
    order = np.arange(MODES)
    top = np.maximum(np.maximum(order[:, None, None], order[None, :, None]), order[None, None, :])
    column = np.full((ROWS, LANES), 99, np.int32)
    column[: MODES**3] = top.reshape(-1)[:, None]
    return jnp.asarray(column)


def split(array):
    high = array.astype(BF16)
    return high, (array - high.astype(F32)).astype(BF16)


def product(table_ref, *pieces):
    stacked = jnp.concatenate(pieces, axis=0)
    return jnp.dot(table_ref[...], stacked, preferred_element_type=F32)


def take(table, index):
    row, lane = index >> 7, index & (LANES - 1)
    result = jnp.zeros_like(table)
    for s in range(table.shape[0]):
        line = jnp.broadcast_to(table[s : s + 1, :], table.shape)
        result = jnp.where(row == s, jnp.take_along_axis(line, lane, axis=1), result)
    return result


def arrange(
    devices, capacity, coef_ref, degree_ref, new_degree_ref, link_ref, owner_ref, top_ref,
    start_ref, aux_ref, flat_ref, pair_ref,
):
    rows = SIDE
    count = rows * LANES
    iota = lax.broadcasted_iota
    sub, lane = iota(jnp.int32, (rows, LANES), 0), iota(jnp.int32, (rows, LANES), 1)
    own = sub * LANES + lane
    links = [
        jnp.concatenate(
            [link_ref[face : face + 1, b * LANES : (b + 1) * LANES] for b in range(rows)], axis=0
        )
        for face in range(6)
    ]
    inside = [(link >= 0) & (link < count) for link in links]
    corner = ~(inside[0] | inside[2] | inside[4])
    first = jnp.sum(jnp.where(corner, own, 0).astype(F32), axis=1, keepdims=True)
    first = jnp.sum(first, axis=0, keepdims=True).astype(jnp.int32)
    order = jnp.broadcast_to(first, (rows, LANES))
    for face, place, bits in ((3, lane & (DEPTH - 1), 4), (5, lane >> 4, 3), (1, sub, 3)):
        step = jnp.where(inside[face], links[face], own)
        for bit in range(bits):
            order = jnp.where(((place >> bit) & 1) == 1, take(step, order), order)
            if bit < bits - 1:
                step = take(step, step)
    owner = owner_ref[...]
    before = (iota(jnp.int32, (LANES, LANES), 0) < iota(jnp.int32, (LANES, LANES), 1)).astype(F32)
    before = before.astype(BF16)
    base = jnp.zeros((devices, 1), F32)
    lines = []
    for b in range(rows):
        named = (iota(jnp.int32, (devices, LANES), 0) == owner[b : b + 1, :]).astype(F32)
        earlier = jnp.dot(named.astype(BF16), before, preferred_element_type=F32) + base
        lines.append(jnp.sum(named * earlier, axis=0, keepdims=True))
        base = base + jnp.sum(named, axis=1, keepdims=True)
    rank = jnp.concatenate(lines, axis=0).astype(jnp.int32)
    column = take(owner * capacity + rank, order)
    degree = take(degree_ref[...], order)
    new_degree = take(new_degree_ref[...], order)
    aux_ref[...] = jnp.zeros_like(aux_ref)
    for b in range(rows):
        at = slice(b * LANES, (b + 1) * LANES)
        for row, array in enumerate((degree, new_degree, column, order)):
            aux_ref[row : row + 1, at] = array[b : b + 1, :]
    flat_ref[ROWS - 16 :, :] = jnp.zeros((16, count), F32)
    for i in range(MODES):
        for j in range(MODES):
            at = (i * MODES + j) * MODES
            flat_ref[at : at + MODES, :] = coef_ref[i, j]
    high, low = split(flat_ref[...])
    pair_ref[:ROWS, :] = high
    pair_ref[ROWS:, :] = low
    top = top_ref[:, :1]

    def body(c, carry):
        at = pl.ds(pl.multiple_of(c * WORK, WORK), WORK)
        chooser = (iota(jnp.int32, (count, WORK), 0) == aux_ref[3:4, at]).astype(F32).astype(BF16)
        both = jnp.dot(pair_ref[...], chooser, preferred_element_type=F32)
        mask = top <= aux_ref[0:1, at]
        start_ref[:, at] = jnp.where(mask, both[:ROWS] + both[ROWS:], 0.0)
        return carry

    lax.fori_loop(0, count // WORK, body, 0)


def evolve(
    wide, narrow, capacity, aux_ref, top_ref, rates_ref, start_at, eval_at, back_at, trace_at, gather_at,
    moved_ref,
    start_ref, eval_ref, back_ref, trace_ref, gather_ref, table_sem, recv_ref, flat_ref, state_ref, face_refs, up_ref, down_ref, both_ref, pair_ref, send_ref,
    z_out, z_in, halo_send, halo_recv, send_sem, recv_sem,
):
    devices = wide * narrow
    count = start_ref.shape[1]
    w, n = lax.axis_index("wide"), lax.axis_index("narrow")
    me = w * narrow + n
    barrier = pltpu.get_barrier_semaphore()
    pairs = ((start_at, start_ref), (eval_at, eval_ref), (back_at, back_ref))
    pairs = pairs + ((trace_at, trace_ref), (gather_at, gather_ref))
    loads = [
        pltpu.make_async_copy(source, target, table_sem.at[i])
        for i, (source, target) in enumerate(pairs)
    ]
    for load in loads:
        load.start()

    def greet(k, carry):
        other = lax.rem(me + k, devices)
        pl.semaphore_signal(
            barrier, inc=1, device_id=(other // narrow, lax.rem(other, narrow)), device_id_type=MESH
        )
        return carry

    lax.fori_loop(1, devices, greet, 0)
    top = top_ref[:, :1]
    half = TRACE + ROWS
    iota = lax.broadcasted_iota
    lane = iota(jnp.int32, (PAIR, LANES), 1)
    flip = jnp.where(iota(jnp.int32, (PAIR, LANES), 0) < FACE, -1.0, 1.0)

    def local_part(source_ref):
        def body(c, carry):
            at = pl.ds(pl.multiple_of(c * WORK, WORK), WORK)
            high, low = split(source_ref[:, at])
            values = product(eval_ref, high, low, high)
            values = values + values * values * values * (1.0 / 3.0)
            high, low = split(values)
            field = product(back_ref, high, low, high)
            field = jnp.where(top <= aux_ref[0:1, at], field, 0.0)
            high, low = split(field)
            both_ref[TRACE:half, at] = high
            both_ref[half + TRACE :, at] = low
            traces = product(trace_ref, high, low)
            down_ref[:, at] = traces[:PAIR]
            up_ref[:, pl.ds(pl.multiple_of(c * WORK + LANES, LANES), WORK)] = traces[
                PAIR : 2 * PAIR
            ]
            for face in range(2, 6):
                face_refs[face - 2, :, at] = traces[face * PAIR : (face + 1) * PAIR]
            return carry

        lax.fori_loop(0, count // WORK, body, 0)

    def exchange(turn):
        low_side = jnp.zeros((PAIR, LANES), F32)
        high_side = jnp.zeros((PAIR, LANES), F32)
        for b in range(SIDE):
            at = slice(b * LANES, (b + 1) * LANES)
            mine = (lane >> 4) == b
            lower = face_refs[2, :, at]
            upper = face_refs[3, :, at]
            shift = b * DEPTH
            low_side = jnp.where(mine, pltpu.roll(lower, shift, 1) if shift else lower, low_side)
            shift = (b * DEPTH + DEPTH) % LANES
            high_side = jnp.where(mine, pltpu.roll(upper, shift, 1) if shift else upper, high_side)
        z_out[turn, 0] = low_side
        z_out[turn, 1] = high_side
        plans = (
            (w > 0, z_out.at[turn, 2], z_in.at[turn, 3], (w - 1, n)),
            (w < wide - 1, z_out.at[turn, 3], z_in.at[turn, 2], (w + 1, n)),
            (n > 0, z_out.at[turn, 0], z_in.at[turn, 1], (w, n - 1)),
            (n < narrow - 1, z_out.at[turn, 1], z_in.at[turn, 0], (w, n + 1)),
        )
        z_out[turn, 2] = down_ref[:, 0:LANES]
        z_out[turn, 3] = up_ref[:, count : count + LANES]
        into = (3, 2, 1, 0)
        side_of = (2, 3, 0, 1)

        def copy(k):
            return pltpu.make_async_remote_copy(
                src_ref=plans[k][1],
                dst_ref=plans[k][2],
                send_sem=halo_send.at[turn, k],
                recv_sem=halo_recv.at[turn, into[k]],
                device_id=plans[k][3],
                device_id_type=MESH,
            )

        for k in range(4):
            pl.when(plans[k][0])(lambda k=k: copy(k).start())

        def finish():
            for k in range(4):
                slot = side_of[k]

                def arrive(k=k, slot=slot):
                    pltpu.make_async_remote_copy(
                        src_ref=plans[k][1],
                        dst_ref=z_in.at[turn, slot],
                        send_sem=halo_send.at[turn, k],
                        recv_sem=halo_recv.at[turn, slot],
                        device_id=plans[k][3],
                        device_id_type=MESH,
                    ).wait()

                def mirror(slot=slot):
                    z_in[turn, slot] = z_out[turn, slot] * flip

                pl.when(plans[k][0])(arrive)
                pl.when(jnp.logical_not(plans[k][0]))(mirror)
            up_ref[:, 0:LANES] = z_in[turn, 2]
            down_ref[:, count : count + LANES] = z_in[turn, 3]

        return finish

    def terms(turn, b, faces):
        at = slice(b * LANES, (b + 1) * LANES)
        later = slice((b + 1) * LANES, (b + 2) * LANES)
        sigma = (aux_ref[0:1, at] + 1).astype(F32)
        sigma = sigma * sigma
        for face in faces:
            sign = 2.0 * (face % 2) - 1.0
            if face == 0:
                own, ghost = down_ref[:, at], up_ref[:, at]
            elif face == 1:
                own, ghost = up_ref[:, later], down_ref[:, later]
            else:
                own, other = face_refs[face - 2, :, at], face_refs[(face ^ 1) - 2, :, at]
                if face == 2:
                    edge, ghost = (lane & (DEPTH - 1)) == 0, pltpu.roll(other, 1, 1)
                    outer = own * flip
                elif face == 3:
                    edge, ghost = (lane & (DEPTH - 1)) == DEPTH - 1, pltpu.roll(other, LANES - 1, 1)
                    outer = own * flip
                elif face == 4:
                    edge, ghost = (lane >> 4) == 0, pltpu.roll(other, DEPTH, 1)
                    shift = (LANES - b * DEPTH) % LANES
                    outer = z_in[turn, 0]
                    outer = pltpu.roll(outer, shift, 1) if shift else outer
                else:
                    edge, ghost = (lane >> 4) == SIDE - 1, pltpu.roll(other, LANES - DEPTH, 1)
                    shift = (LANES - DEPTH - b * DEPTH) % LANES
                    outer = z_in[turn, 1]
                    outer = pltpu.roll(outer, shift, 1) if shift else outer
                ghost = jnp.where(edge, outer, ghost)
            jump = own[:FACE] - ghost[:FACE]
            sums = own[FACE:] + ghost[FACE:]
            base = face * PAIR
            both = jnp.concatenate(
                [(0.5 * sign) * sums - sigma * jump, (1.5 * sign) * jump], axis=0
            )
            high, low = split(both)
            both_ref[base : base + PAIR, at] = high
            both_ref[half + base : half + base + PAIR, at] = low

    def residual(c):
        at = pl.ds(pl.multiple_of(c * WORK, WORK), WORK)
        change = jnp.dot(gather_ref[...], both_ref[:, at], preferred_element_type=F32)
        field = both_ref[TRACE:half, at].astype(F32) + both_ref[half + TRACE :, at].astype(F32)
        change = change * rates_ref[0, :, :1] + field * rates_ref[1, :, :1]
        return at, jnp.where(top <= aux_ref[0:1, at], change, 0.0)

    def section(turn, source_ref, before_send, store):
        local_part(source_ref)
        before_send()
        finish = exchange(turn)
        for b in range(SIDE):
            terms(turn, b, (2, 3))
        finish()
        for b in range(SIDE):
            terms(turn, b, (0, 1, 4, 5))
        lax.fori_loop(0, count // WORK, store, 0)

    def enter():
        loads[4].wait()
        pl.semaphore_wait(barrier, devices - 1)

    def store_first(c, carry):
        at, change = residual(c)
        state_ref[:, at] = start_ref[:, at] + change
        return carry

    def store_second(c, carry):
        at, change = residual(c)
        second = 0.5 * (start_ref[:, at] + state_ref[:, at] + change)
        high, low = split(jnp.where(top <= aux_ref[1:2, at], second, 0.0))
        pair_ref[:ROWS, at] = high
        pair_ref[ROWS:, at] = low
        return carry

    for load in loads[:4]:
        load.wait()
    section(0, start_ref, enter, store_first)
    section(1, state_ref, lambda: None, store_second)

    share = LANES // capacity
    height = send_ref.shape[1]
    tiles = devices * capacity // LANES
    first_tile = me // share + 1
    wide_lane = iota(jnp.int32, (height, LANES), 1)

    def outgoing(other):
        return pltpu.make_async_remote_copy(
            src_ref=send_ref.at[other],
            dst_ref=recv_ref.at[me],
            send_sem=send_sem.at[other],
            recv_sem=recv_sem.at[me],
            device_id=(other // narrow, lax.rem(other, narrow)),
            device_id_type=MESH,
        )

    def place(t, carry):
        tile = lax.rem(first_tile + t, tiles)
        slot = iota(jnp.int32, (LANES, count), 0) + tile * LANES
        chooser = (slot == aux_ref[2:3, :]).astype(F32).astype(BF16)
        both = lax.dot_general(
            pair_ref[...], chooser, (((1,), (1,)), ((), ())), preferred_element_type=F32
        )
        columns = both[:ROWS] + both[ROWS:]
        if share * height > ROWS:
            columns = jnp.concatenate(
                [columns, jnp.zeros((share * height - ROWS, LANES), F32)], axis=0
            )
        for j in range(share):
            block = jnp.zeros((height, LANES), F32)
            for q in range(share):
                piece = columns[q * height : (q + 1) * height]
                shift = ((q - j) * capacity) % LANES
                piece = pltpu.roll(piece, shift, 1) if shift else piece
                block = jnp.where(wide_lane // capacity == q, piece, block)
            other = tile * share + j

            @pl.when(other == me)
            def _(block=block):
                recv_ref[me] = block

            @pl.when(other != me)
            def _(block=block, other=other):
                send_ref[other] = block
                outgoing(other).start()

        return carry

    lax.fori_loop(0, tiles, place, 0)

    def collect(t, carry):
        tile = lax.rem(first_tile + tiles - t, tiles)
        pieces = [jnp.zeros((height, LANES), F32) for _ in range(share)]
        for j in range(share):
            source = tile * share + j

            @pl.when(source != me)
            def _(source=source):
                pltpu.make_async_remote_copy(
                    src_ref=send_ref.at[source],
                    dst_ref=recv_ref.at[source],
                    send_sem=send_sem.at[source],
                    recv_sem=recv_sem.at[source],
                    device_id=(source // narrow, lax.rem(source, narrow)),
                    device_id_type=MESH,
                ).wait()

            block = recv_ref[source]
            for q in range(share):
                shift = ((j - q) * capacity) % LANES
                moved = pltpu.roll(block, shift, 1) if shift else block
                pieces[q] = jnp.where(wide_lane // capacity == j, moved, pieces[q])
        for q in range(share):
            flat_ref[q * height : (q + 1) * height, :] = pieces[q]
        at = pl.ds(pl.multiple_of(tile * LANES, LANES), LANES)
        for i in range(MODES):
            for j in range(MODES):
                row = (i * MODES + j) * MODES
                moved_ref[i, j, :, at] = flat_ref[row : row + MODES, :]
        return carry

    lax.fori_loop(0, tiles, collect, 0)


def on_device(coefficients, degree, new_degree, face_link, send_index, new_owner):
    wide, narrow = lax.axis_size("wide"), lax.axis_size("narrow")
    devices = wide * narrow
    count = coefficients.shape[3]
    capacity = max(2, 2 * count // devices)
    share = LANES // capacity
    modes = MODES**3
    height = -(-(-(-modes // share)) // 8) * 8
    evaluate, back, trace, gather, rates = operators()
    top = highest_modes()
    vmem = pl.BlockSpec(memory_space=pltpu.VMEM)
    square = (SIDE, LANES)
    start, aux = pl.pallas_call(
        functools.partial(arrange, devices, capacity),
        out_shape=(
            jax.ShapeDtypeStruct((ROWS, count), F32),
            jax.ShapeDtypeStruct((8, count), jnp.int32),
        ),
        in_specs=[vmem] * 6,
        out_specs=(vmem, vmem),
        scratch_shapes=[pltpu.VMEM((ROWS, count), F32), pltpu.VMEM((2 * ROWS, count), BF16)],
        compiler_params=pltpu.CompilerParams(vmem_limit_bytes=48 * 2**20),
        name="arrange",
    )(
        coefficients,
        degree.reshape(square),
        new_degree.reshape(square),
        face_link,
        new_owner.reshape(square),
        top,
    )
    anywhere = pl.BlockSpec(memory_space=pl.ANY)
    return pl.pallas_call(
        functools.partial(evolve, wide, narrow, capacity),
        out_shape=jax.ShapeDtypeStruct((MODES, MODES, MODES, devices * capacity), F32),
        in_specs=[vmem] * 3 + [anywhere] * 5,
        out_specs=vmem,
        scratch_shapes=[
            pltpu.VMEM((ROWS, count), F32),
            pltpu.VMEM(evaluate.shape, BF16),
            pltpu.VMEM(back.shape, BF16),
            pltpu.VMEM(trace.shape, BF16),
            pltpu.VMEM(gather.shape, BF16),
            pltpu.SemaphoreType.DMA((5,)),
            pltpu.VMEM((devices, height, LANES), F32),
            pltpu.VMEM((share * height, LANES), F32),
            pltpu.VMEM((ROWS, count), F32),
            pltpu.VMEM((4, PAIR, count), F32),
            pltpu.VMEM((PAIR, count + LANES), F32),
            pltpu.VMEM((PAIR, count + LANES), F32),
            pltpu.VMEM((2 * (TRACE + ROWS), count), BF16),
            pltpu.VMEM((2 * ROWS, count), BF16),
            pltpu.VMEM((devices, height, LANES), F32),
            pltpu.VMEM((2, 4, PAIR, LANES), F32),
            pltpu.VMEM((2, 4, PAIR, LANES), F32),
            pltpu.SemaphoreType.DMA((2, 4)),
            pltpu.SemaphoreType.DMA((2, 4)),
            pltpu.SemaphoreType.DMA((devices,)),
            pltpu.SemaphoreType.DMA((devices,)),
        ],
        compiler_params=pltpu.CompilerParams(
            collective_id=0, has_side_effects=True, vmem_limit_bytes=36 * 2**20
        ),
        name="evolve",
    )(aux, top, rates, start, evaluate, back, trace, gather)


def solution(mesh):
    placed = (
        P(None, None, None, ("wide", "narrow")),
        P(("wide", "narrow")),
        P(("wide", "narrow")),
        P(None, ("wide", "narrow")),
        P(None, ("wide", "narrow")),
        P(("wide", "narrow"), None),
    )
    return jax.shard_map(
        on_device,
        mesh=mesh,
        in_specs=placed,
        out_specs=P(None, None, None, ("wide", "narrow")),
        check_vma=False,
    )
```

```python
import functools

import jax
import jax.numpy as jnp
import numpy as np
from jax import lax
from jax.experimental import pallas as pl
from jax.experimental.pallas import tpu as pltpu
from jax.sharding import PartitionSpec as P

MODES = 7
QUAD = 8
SIDE = 8
DEPTH = 16
LANES = 128
ROWS = 352
FACE = 56
PAIR = 2 * FACE
TRACE = 6 * PAIR
WORK = 512
STEP_SIZE = 0.0003
MESH = pl.DeviceIdType.MESH
F32 = jnp.float32
BF16 = jnp.bfloat16


def legendre_rows(points, count):
    values = [points * 0.0 + 1.0, points.copy()]
    slopes = [points * 0.0, points * 0.0 + 1.0]
    for order in range(1, count):
        values.append(
            ((2.0 * order + 1.0) * points * values[order] - order * values[order - 1])
            / (order + 1.0)
        )
        slopes.append(slopes[order - 1] + (2.0 * order + 1.0) * values[order])
    return (np.stack(values[: count + 1]), np.stack(slopes[: count + 1]))


def gauss_rule(count):
    points = np.cos(np.pi * (np.arange(count) + 0.75) / (count + 0.5))
    for sweep in range(60):
        values, slopes = legendre_rows(points, count)
        points = points - values[count] / slopes[count]
    values, slopes = legendre_rows(points, count)
    weights = 2.0 / ((1.0 - points * points) * slopes[count] ** 2)
    return (points[::-1], weights[::-1])


def operators():
    points, weights = gauss_rule(QUAD)
    scales = np.sqrt((2.0 * np.arange(MODES) + 1.0) / 2.0)
    value_rows, slope_rows = legendre_rows(points, MODES)
    values = value_rows[:MODES].T * scales
    slopes = slope_rows[:MODES].T * scales
    stiffness = slopes.T @ (weights[:, None] * slopes)
    project = (values * weights[:, None]).T
    orders = np.arange(MODES)
    ends = np.stack([(-1.0) ** orders, np.ones(MODES)]) * scales
    end_slopes = (
        np.stack([(-1.0) ** (orders + 1), np.ones(MODES)]) * (orders * (orders + 1) / 2.0) * scales
    )
    eye = np.eye(MODES)
    scaled = np.ones(ROWS)
    scaled[: MODES**3] = np.kron(scales, np.kron(scales, scales))

    def kron(first, second, third):
        return np.kron(first, np.kron(second, third))

    modes = MODES**3
    evaluate = np.zeros((QUAD**3, ROWS))
    evaluate[:, :modes] = kron(values, values, values)
    back = np.zeros((ROWS, QUAD**3))
    back[:modes] = kron(project, project, project)
    back = back * scaled[:, None]
    gather = np.zeros((ROWS, TRACE + ROWS))
    trace = np.zeros((TRACE, ROWS))
    plane = MODES**2
    for face in range(6):
        axis, side = divmod(face, 2)
        for kind, vector in enumerate((ends[side], end_slopes[side])):
            parts = [eye, eye, eye]
            parts[axis] = (vector / scales)[None, :]
            base = face * PAIR + kind * FACE
            trace[base : base + plane, :modes] = kron(*parts)
            parts[axis] = (vector * scales / (1.0, 3.0)[kind])[:, None]
            gather[:modes, base : base + plane] = kron(*parts)
    inner = kron(stiffness, eye, eye) + kron(eye, stiffness, eye) + kron(eye, eye, stiffness)
    diagonal = np.zeros(ROWS)
    diagonal[:modes] = -np.diag(inner)
    ratio = scaled[:modes, None] / scaled[None, :modes]
    gather[:modes, TRACE : TRACE + modes] = (np.diag(np.diag(inner)) - inner) * ratio
    rates = STEP_SIZE * np.stack([1.0 / scaled, diagonal / scaled])
    rates = np.repeat(rates[:, :, None], LANES, axis=2).astype(np.float32)
    return thrice(evaluate), thrice(back), twice(trace), twice(gather), jnp.asarray(rates)


def thrice(array):
    high = array.astype(jnp.bfloat16)
    low = (array - high.astype(np.float64)).astype(jnp.bfloat16)
    return jnp.asarray(np.concatenate([high, high, low], axis=1))


def twice(array):
    high = array.astype(jnp.bfloat16)
    assert np.abs(high.astype(np.float64) - array).max() < 1e-9
    return jnp.asarray(np.concatenate([high, high], axis=1))


def highest_modes():
    order = np.arange(MODES)
    top = np.maximum(np.maximum(order[:, None, None], order[None, :, None]), order[None, None, :])
    column = np.full((ROWS, LANES), 99, np.int32)
    column[: MODES**3] = top.reshape(-1)[:, None]
    return jnp.asarray(column)


def split(array):
    high = array.astype(BF16)
    return high, (array - high.astype(F32)).astype(BF16)


def product(table_ref, *pieces):
    stacked = jnp.concatenate(pieces, axis=0)
    return jnp.dot(table_ref[...], stacked, preferred_element_type=F32)


def take(table, index):
    row, lane = index >> 7, index & (LANES - 1)
    result = jnp.zeros_like(table)
    for s in range(table.shape[0]):
        line = jnp.broadcast_to(table[s : s + 1, :], table.shape)
        result = jnp.where(row == s, jnp.take_along_axis(line, lane, axis=1), result)
    return result


def arrange(
    devices, capacity, coef_ref, degree_ref, new_degree_ref, link_ref, owner_ref, top_ref,
    start_ref, aux_ref, flat_ref, pair_ref,
):
    rows = SIDE
    count = rows * LANES
    iota = lax.broadcasted_iota
    sub, lane = iota(jnp.int32, (rows, LANES), 0), iota(jnp.int32, (rows, LANES), 1)
    own = sub * LANES + lane
    links = [
        jnp.concatenate(
            [link_ref[face : face + 1, b * LANES : (b + 1) * LANES] for b in range(rows)], axis=0
        )
        for face in range(6)
    ]
    inside = [(link >= 0) & (link < count) for link in links]
    corner = ~(inside[0] | inside[2] | inside[4])
    first = jnp.sum(jnp.where(corner, own, 0).astype(F32), axis=1, keepdims=True)
    first = jnp.sum(first, axis=0, keepdims=True).astype(jnp.int32)
    order = jnp.broadcast_to(first, (rows, LANES))
    for face, place, bits in ((3, lane & (DEPTH - 1), 4), (5, lane >> 4, 3), (1, sub, 3)):
        step = jnp.where(inside[face], links[face], own)
        for bit in range(bits):
            order = jnp.where(((place >> bit) & 1) == 1, take(step, order), order)
            if bit < bits - 1:
                step = take(step, step)
    owner = owner_ref[...]
    before = (iota(jnp.int32, (LANES, LANES), 0) < iota(jnp.int32, (LANES, LANES), 1)).astype(F32)
    before = before.astype(BF16)
    base = jnp.zeros((devices, 1), F32)
    lines = []
    for b in range(rows):
        named = (iota(jnp.int32, (devices, LANES), 0) == owner[b : b + 1, :]).astype(F32)
        earlier = jnp.dot(named.astype(BF16), before, preferred_element_type=F32) + base
        lines.append(jnp.sum(named * earlier, axis=0, keepdims=True))
        base = base + jnp.sum(named, axis=1, keepdims=True)
    rank = jnp.concatenate(lines, axis=0).astype(jnp.int32)
    column = take(owner * capacity + rank, order)
    degree = take(degree_ref[...], order)
    new_degree = take(new_degree_ref[...], order)
    aux_ref[...] = jnp.zeros_like(aux_ref)
    for b in range(rows):
        at = slice(b * LANES, (b + 1) * LANES)
        for row, array in enumerate((degree, new_degree, column, order)):
            aux_ref[row : row + 1, at] = array[b : b + 1, :]
    flat_ref[ROWS - 16 :, :] = jnp.zeros((16, count), F32)
    for i in range(MODES):
        for j in range(MODES):
            at = (i * MODES + j) * MODES
            flat_ref[at : at + MODES, :] = coef_ref[i, j]
    high, low = split(flat_ref[...])
    pair_ref[:ROWS, :] = high
    pair_ref[ROWS:, :] = low
    top = top_ref[:, :1]

    def body(c, carry):
        at = pl.ds(pl.multiple_of(c * WORK, WORK), WORK)
        chooser = (iota(jnp.int32, (count, WORK), 0) == aux_ref[3:4, at]).astype(F32).astype(BF16)
        both = jnp.dot(pair_ref[...], chooser, preferred_element_type=F32)
        mask = top <= aux_ref[0:1, at]
        start_ref[:, at] = jnp.where(mask, both[:ROWS] + both[ROWS:], 0.0)
        return carry

    lax.fori_loop(0, count // WORK, body, 0)


def evolve(
    wide, narrow, capacity, aux_ref, top_ref, rates_ref, start_at, eval_at, back_at, trace_at, gather_at,
    moved_ref,
    start_ref, eval_ref, back_ref, trace_ref, gather_ref, table_sem, recv_ref, flat_ref, state_ref, face_refs, up_ref, down_ref, both_ref, pair_ref, send_ref,
    z_out, z_in, halo_send, halo_recv, send_sem, recv_sem,
):
    devices = wide * narrow
    count = start_ref.shape[1]
    w, n = lax.axis_index("wide"), lax.axis_index("narrow")
    me = w * narrow + n
    barrier = pltpu.get_barrier_semaphore()
    pairs = ((start_at, start_ref), (eval_at, eval_ref), (back_at, back_ref))
    pairs = pairs + ((trace_at, trace_ref), (gather_at, gather_ref))
    loads = [
        pltpu.make_async_copy(source, target, table_sem.at[i])
        for i, (source, target) in enumerate(pairs)
    ]
    for load in loads:
        load.start()

    def greet(k, carry):
        other = lax.rem(me + k, devices)
        pl.semaphore_signal(
            barrier, inc=1, device_id=(other // narrow, lax.rem(other, narrow)), device_id_type=MESH
        )
        return carry

    lax.fori_loop(1, devices, greet, 0)
    top = top_ref[:, :1]
    half = TRACE + ROWS
    iota = lax.broadcasted_iota
    lane = iota(jnp.int32, (PAIR, LANES), 1)
    flip = jnp.where(iota(jnp.int32, (PAIR, LANES), 0) < FACE, -1.0, 1.0)

    def local_part(source_ref):
        def body(c, carry):
            at = pl.ds(pl.multiple_of(c * WORK, WORK), WORK)
            high, low = split(source_ref[:, at])
            values = product(eval_ref, high, low, high)
            values = values + values * values * values * (1.0 / 3.0)
            high, low = split(values)
            field = product(back_ref, high, low, high)
            field = jnp.where(top <= aux_ref[0:1, at], field, 0.0)
            high, low = split(field)
            both_ref[TRACE:half, at] = high
            both_ref[half + TRACE :, at] = low
            traces = product(trace_ref, high, low)
            down_ref[:, at] = traces[:PAIR]
            up_ref[:, pl.ds(pl.multiple_of(c * WORK + LANES, LANES), WORK)] = traces[
                PAIR : 2 * PAIR
            ]
            for face in range(2, 6):
                face_refs[face - 2, :, at] = traces[face * PAIR : (face + 1) * PAIR]
            return carry

        lax.fori_loop(0, count // WORK, body, 0)

    def exchange(turn):
        low_side = jnp.zeros((PAIR, LANES), F32)
        high_side = jnp.zeros((PAIR, LANES), F32)
        for b in range(SIDE):
            at = slice(b * LANES, (b + 1) * LANES)
            mine = (lane >> 4) == b
            lower = face_refs[2, :, at]
            upper = face_refs[3, :, at]
            shift = b * DEPTH
            low_side = jnp.where(mine, pltpu.roll(lower, shift, 1) if shift else lower, low_side)
            shift = (b * DEPTH + DEPTH) % LANES
            high_side = jnp.where(mine, pltpu.roll(upper, shift, 1) if shift else upper, high_side)
        z_out[turn, 0] = low_side
        z_out[turn, 1] = high_side
        plans = (
            (w > 0, z_out.at[turn, 2], z_in.at[turn, 3], (w - 1, n)),
            (w < wide - 1, z_out.at[turn, 3], z_in.at[turn, 2], (w + 1, n)),
            (n > 0, z_out.at[turn, 0], z_in.at[turn, 1], (w, n - 1)),
            (n < narrow - 1, z_out.at[turn, 1], z_in.at[turn, 0], (w, n + 1)),
        )
        z_out[turn, 2] = down_ref[:, 0:LANES]
        z_out[turn, 3] = up_ref[:, count : count + LANES]
        into = (3, 2, 1, 0)
        side_of = (2, 3, 0, 1)

        def copy(k):
            return pltpu.make_async_remote_copy(
                src_ref=plans[k][1],
                dst_ref=plans[k][2],
                send_sem=halo_send.at[turn, k],
                recv_sem=halo_recv.at[turn, into[k]],
                device_id=plans[k][3],
                device_id_type=MESH,
            )

        for k in range(4):
            pl.when(plans[k][0])(lambda k=k: copy(k).start())

        def finish():
            for k in range(4):
                slot = side_of[k]

                def arrive(k=k, slot=slot):
                    pltpu.make_async_remote_copy(
                        src_ref=plans[k][1],
                        dst_ref=z_in.at[turn, slot],
                        send_sem=halo_send.at[turn, k],
                        recv_sem=halo_recv.at[turn, slot],
                        device_id=plans[k][3],
                        device_id_type=MESH,
                    ).wait()

                def mirror(slot=slot):
                    z_in[turn, slot] = z_out[turn, slot] * flip

                pl.when(plans[k][0])(arrive)
                pl.when(jnp.logical_not(plans[k][0]))(mirror)
            up_ref[:, 0:LANES] = z_in[turn, 2]
            down_ref[:, count : count + LANES] = z_in[turn, 3]

        return finish

    def terms(turn, b, faces):
        at = slice(b * LANES, (b + 1) * LANES)
        later = slice((b + 1) * LANES, (b + 2) * LANES)
        sigma = (aux_ref[0:1, at] + 1).astype(F32)
        sigma = sigma * sigma
        for face in faces:
            sign = 2.0 * (face % 2) - 1.0
            if face == 0:
                own, ghost = down_ref[:, at], up_ref[:, at]
            elif face == 1:
                own, ghost = up_ref[:, later], down_ref[:, later]
            else:
                own, other = face_refs[face - 2, :, at], face_refs[(face ^ 1) - 2, :, at]
                if face == 2:
                    edge, ghost = (lane & (DEPTH - 1)) == 0, pltpu.roll(other, 1, 1)
                    outer = own * flip
                elif face == 3:
                    edge, ghost = (lane & (DEPTH - 1)) == DEPTH - 1, pltpu.roll(other, LANES - 1, 1)
                    outer = own * flip
                elif face == 4:
                    edge, ghost = (lane >> 4) == 0, pltpu.roll(other, DEPTH, 1)
                    shift = (LANES - b * DEPTH) % LANES
                    outer = z_in[turn, 0]
                    outer = pltpu.roll(outer, shift, 1) if shift else outer
                else:
                    edge, ghost = (lane >> 4) == SIDE - 1, pltpu.roll(other, LANES - DEPTH, 1)
                    shift = (LANES - DEPTH - b * DEPTH) % LANES
                    outer = z_in[turn, 1]
                    outer = pltpu.roll(outer, shift, 1) if shift else outer
                ghost = jnp.where(edge, outer, ghost)
            jump = own[:FACE] - ghost[:FACE]
            sums = own[FACE:] + ghost[FACE:]
            base = face * PAIR
            both = jnp.concatenate(
                [(0.5 * sign) * sums - sigma * jump, (1.5 * sign) * jump], axis=0
            )
            high, low = split(both)
            both_ref[base : base + PAIR, at] = high
            both_ref[half + base : half + base + PAIR, at] = low

    def residual(c):
        at = pl.ds(pl.multiple_of(c * WORK, WORK), WORK)
        change = jnp.dot(gather_ref[...], both_ref[:, at], preferred_element_type=F32)
        field = both_ref[TRACE:half, at].astype(F32) + both_ref[half + TRACE :, at].astype(F32)
        change = change * rates_ref[0, :, :1] + field * rates_ref[1, :, :1]
        return at, jnp.where(top <= aux_ref[0:1, at], change, 0.0)

    def section(turn, source_ref, before_send, store):
        local_part(source_ref)
        before_send()
        finish = exchange(turn)
        for b in range(SIDE):
            terms(turn, b, (2, 3))
        finish()
        for b in range(SIDE):
            terms(turn, b, (0, 1, 4, 5))
        lax.fori_loop(0, count // WORK, store, 0)

    def enter():
        loads[4].wait()
        pl.semaphore_wait(barrier, devices - 1)

    def store_first(c, carry):
        at, change = residual(c)
        state_ref[:, at] = start_ref[:, at] + change
        return carry

    def store_second(c, carry):
        at, change = residual(c)
        second = 0.5 * (start_ref[:, at] + state_ref[:, at] + change)
        high, low = split(jnp.where(top <= aux_ref[1:2, at], second, 0.0))
        pair_ref[:ROWS, at] = high
        pair_ref[ROWS:, at] = low
        return carry

    for load in loads[:4]:
        load.wait()
    section(0, start_ref, enter, store_first)
    section(1, state_ref, lambda: None, store_second)

    share = LANES // capacity
    height = send_ref.shape[1]
    tiles = devices * capacity // LANES
    first_tile = me // share + 1
    wide_lane = iota(jnp.int32, (height, LANES), 1)

    def outgoing(other):
        return pltpu.make_async_remote_copy(
            src_ref=send_ref.at[other],
            dst_ref=recv_ref.at[me],
            send_sem=send_sem.at[other],
            recv_sem=recv_sem.at[me],
            device_id=(other // narrow, lax.rem(other, narrow)),
            device_id_type=MESH,
        )

    def place(t, carry):
        tile = lax.rem(first_tile + t, tiles)
        slot = iota(jnp.int32, (LANES, count), 0) + tile * LANES
        chooser = (slot == aux_ref[2:3, :]).astype(F32).astype(BF16)
        both = lax.dot_general(
            pair_ref[...], chooser, (((1,), (1,)), ((), ())), preferred_element_type=F32
        )
        columns = both[:ROWS] + both[ROWS:]
        if share * height > ROWS:
            columns = jnp.concatenate(
                [columns, jnp.zeros((share * height - ROWS, LANES), F32)], axis=0
            )
        for j in range(share):
            block = jnp.zeros((height, LANES), F32)
            for q in range(share):
                piece = columns[q * height : (q + 1) * height]
                shift = ((q - j) * capacity) % LANES
                piece = pltpu.roll(piece, shift, 1) if shift else piece
                block = jnp.where(wide_lane // capacity == q, piece, block)
            other = tile * share + j

            @pl.when(other == me)
            def _(block=block):
                recv_ref[me] = block

            @pl.when(other != me)
            def _(block=block, other=other):
                send_ref[other] = block
                outgoing(other).start()

        return carry

    lax.fori_loop(0, tiles, place, 0)

    def collect(t, carry):
        tile = lax.rem(first_tile + tiles - t, tiles)
        pieces = [jnp.zeros((height, LANES), F32) for _ in range(share)]
        for j in range(share):
            source = tile * share + j

            @pl.when(source != me)
            def _(source=source):
                pltpu.make_async_remote_copy(
                    src_ref=send_ref.at[source],
                    dst_ref=recv_ref.at[source],
                    send_sem=send_sem.at[source],
                    recv_sem=recv_sem.at[source],
                    device_id=(source // narrow, lax.rem(source, narrow)),
                    device_id_type=MESH,
                ).wait()

            block = recv_ref[source]
            for q in range(share):
                shift = ((j - q) * capacity) % LANES
                moved = pltpu.roll(block, shift, 1) if shift else block
                pieces[q] = jnp.where(wide_lane // capacity == j, moved, pieces[q])
        for q in range(share):
            flat_ref[q * height : (q + 1) * height, :] = pieces[q]
        at = pl.ds(pl.multiple_of(tile * LANES, LANES), LANES)
        for i in range(MODES):
            for j in range(MODES):
                row = (i * MODES + j) * MODES
                moved_ref[i, j, :, at] = flat_ref[row : row + MODES, :]
        return carry

    lax.fori_loop(0, tiles, collect, 0)


def on_device(coefficients, degree, new_degree, face_link, send_index, new_owner):
    wide, narrow = lax.axis_size("wide"), lax.axis_size("narrow")
    devices = wide * narrow
    count = coefficients.shape[3]
    capacity = max(2, 2 * count // devices)
    share = LANES // capacity
    modes = MODES**3
    height = -(-(-(-modes // share)) // 8) * 8
    evaluate, back, trace, gather, rates = operators()
    top = highest_modes()
    vmem = pl.BlockSpec(memory_space=pltpu.VMEM)
    square = (SIDE, LANES)
    start, aux = pl.pallas_call(
        functools.partial(arrange, devices, capacity),
        out_shape=(
            jax.ShapeDtypeStruct((ROWS, count), F32),
            jax.ShapeDtypeStruct((8, count), jnp.int32),
        ),
        in_specs=[vmem] * 6,
        out_specs=(vmem, vmem),
        scratch_shapes=[pltpu.VMEM((ROWS, count), F32), pltpu.VMEM((2 * ROWS, count), BF16)],
        compiler_params=pltpu.CompilerParams(vmem_limit_bytes=48 * 2**20),
        name="arrange",
    )(
        coefficients,
        degree.reshape(square),
        new_degree.reshape(square),
        face_link,
        new_owner.reshape(square),
        top,
    )
    anywhere = pl.BlockSpec(memory_space=pl.ANY)
    return pl.pallas_call(
        functools.partial(evolve, wide, narrow, capacity),
        out_shape=jax.ShapeDtypeStruct((MODES, MODES, MODES, devices * capacity), F32),
        in_specs=[vmem] * 3 + [anywhere] * 5,
        out_specs=vmem,
        scratch_shapes=[
            pltpu.VMEM((ROWS, count), F32),
            pltpu.VMEM(evaluate.shape, BF16),
            pltpu.VMEM(back.shape, BF16),
            pltpu.VMEM(trace.shape, BF16),
            pltpu.VMEM(gather.shape, BF16),
            pltpu.SemaphoreType.DMA((5,)),
            pltpu.VMEM((devices, height, LANES), F32),
            pltpu.VMEM((share * height, LANES), F32),
            pltpu.VMEM((ROWS, count), F32),
            pltpu.VMEM((4, PAIR, count), F32),
            pltpu.VMEM((PAIR, count + LANES), F32),
            pltpu.VMEM((PAIR, count + LANES), F32),
            pltpu.VMEM((2 * (TRACE + ROWS), count), BF16),
            pltpu.VMEM((2 * ROWS, count), BF16),
            pltpu.VMEM((devices, height, LANES), F32),
            pltpu.VMEM((2, 4, PAIR, LANES), F32),
            pltpu.VMEM((2, 4, PAIR, LANES), F32),
            pltpu.SemaphoreType.DMA((2, 4)),
            pltpu.SemaphoreType.DMA((2, 4)),
            pltpu.SemaphoreType.DMA((devices,)),
            pltpu.SemaphoreType.DMA((devices,)),
        ],
        compiler_params=pltpu.CompilerParams(
            collective_id=0, has_side_effects=True, vmem_limit_bytes=36 * 2**20
        ),
        name="evolve",
    )(aux, top, rates, start, evaluate, back, trace, gather)


def solution(mesh):
    placed = (
        P(None, None, None, ("wide", "narrow")),
        P(("wide", "narrow")),
        P(("wide", "narrow")),
        P(None, ("wide", "narrow")),
        P(None, ("wide", "narrow")),
        P(("wide", "narrow"), None),
    )
    return jax.shard_map(
        on_device,
        mesh=mesh,
        in_specs=placed,
        out_specs=P(None, None, None, ("wide", "narrow")),
        check_vma=False,
    )
```
